32 devices in a mesh: seq: 8 (over z, x), head: 4 (over y, core).
Axes of the slice: x: 2, y: 2, z: 4, core: 2. Of those that a mesh axis runs over, the one named last changes fastest.
Arguments:
- inputs: bfloat16 [4096, 1024], P('seq', 'head'), may hold values from -6 to 6
- lengths: int32 [8], replicated, may hold values from 1 to 4089, as said below
- norm1_gain: bfloat16 [1024], P(('head', 'seq')), may hold values from 0.5 to 1.5
- w_in: bfloat16 [1024, 6144], P('seq', 'head'), may hold values from -0.1875 to 0.1875
- w_small: bfloat16 [1024, 24], P('seq', 'head'), may hold values from -0.375 to 0.375
- conv_weight: bfloat16 [4, 5120], P(None, ('head', 'seq')), may hold values from -3 to 3
- decay_rate: float32 [8], P('head'), as said below
- out_gain: bfloat16 [1024], P(('head', 'seq')), may hold values from 0.5 to 1.5
- w_out: bfloat16 [1024, 1024], P('head', 'seq'), may hold values from -0.375 to 0.375
- norm2_gain: bfloat16 [1024], P(('head', 'seq')), may hold values from 0.5 to 1.5
- w_gate: bfloat16 [1024, 2816], P('seq', 'head'), may hold values from -0.1875 to 0.1875
- w_up: bfloat16 [1024, 2816], P('seq', 'head'), may hold values from -0.1875 to 0.1875
- w_down: bfloat16 [2816, 1024], P('head', 'seq'), may hold values from -0.21875 to 0.21875
- cotangent: bfloat16 [4096, 1024], P('seq', 'head'), may hold values from -6 to 6
Outputs:
- output: bfloat16 [4096, 1024], P('seq', 'head')
- grad_inputs: float32 [4096, 1024], P('seq', 'head')
- grad_norm1_gain: float32 [1024], P(('head', 'seq'))
- grad_w_in: float32 [1024, 6144], P('seq', 'head')
- grad_w_small: float32 [1024, 24], P('seq', 'head')
- grad_conv_weight: float32 [4, 5120], P(None, ('head', 'seq'))
- grad_decay_rate: float32 [8], P('head')
- grad_out_gain: float32 [1024], P(('head', 'seq'))
- grad_w_out: float32 [1024, 1024], P('head', 'seq')
- grad_norm2_gain: float32 [1024], P(('head', 'seq'))
- grad_w_gate: float32 [1024, 2816], P('seq', 'head')
- grad_w_up: float32 [1024, 2816], P('seq', 'head')
- grad_w_down: float32 [2816, 1024], P('head', 'seq')
The draws below stay inside these ranges and needn't reach their ends.
Inputs may be any that keep to these rules, and one draw needn't show every extreme that they name: 8 document lengths in token order summing to 4096; one document starts within the first 512 tokens and ends within the last 512; every other one has at most 64 tokens. `decay_rate`: one rate a head, between 0.5 / 4096 and 0.05.
All inputs are finite; a program needn't handle non-finite values.
Results may differ from the reference program's by a relative error of at most 0.02125.
Values may be sent and summed in bfloat16 or wider, within the bound.
A program may use at most 192 MiB of HBM per device.

```python
import math
import jax
import jax.numpy as jnp
from jax import lax

D = 1024
H = 8
HEAD_DIM = 128
FF = 2816
HOUSE = 2
GROUP = 64
TOK_DEV = 512
NDOC = 8
TOKENS = 4096
N_SEQ = 8


def draw_lengths(key, part):
    key = jax.random.fold_in(key, 11)
    key_place, key_level, key_value = jax.random.split(key, 3)
    limit = TOK_DEV // NDOC
    levels = limit.bit_length()
    place = jax.random.randint(key_place, (), 1, NDOC - 1)
    level = jax.random.randint(key_level, (NDOC,), 0, levels)
    ceiling = jnp.minimum(jnp.left_shift(jnp.ones((NDOC,), jnp.int32), level), limit)
    short = jax.random.randint(key_value, (NDOC,), 1, ceiling + 1)
    others = jnp.sum(short) - short[place]
    slots = jnp.arange(NDOC)
    return jnp.where(slots == place, TOKENS - others, short).astype(jnp.int32)


def draw_decay_rate(key, part):
    key = jax.random.fold_in(key, 23)
    fraction = jax.random.uniform(key, (H,), jnp.float32)
    lowest = math.log(0.5 / TOKENS)
    highest = math.log(0.05)
    return jnp.exp(lowest + fraction * (highest - lowest)).astype(jnp.float32)


def level_of(rng, dims, cuts, low, largest):
    def one(axis_at, blocks):
        steps = jax.random.uniform(jax.random.fold_in(jax.random.fold_in(rng, 6), axis_at), (blocks,), jnp.float32, low / len(cuts), largest / len(cuts))
        return jnp.repeat(jnp.exp(steps), dims[axis_at] // blocks).reshape((-1,) + (1,) * (len(dims) - axis_at - 1))

    factor_of = one(*cuts[0])
    for cut in cuts[1:]:
        factor_of = factor_of * one(*cut)
    return factor_of


def scatter_about(rng, shape, scale, bound, cuts=(), kind=jnp.bfloat16):
    factor_of = level_of(rng, shape, cuts, -0.22, 0.18) if cuts else 1.0
    values = jax.random.normal(rng, shape, jnp.float32) * scale * factor_of
    return jnp.minimum(jnp.maximum(values, -bound), bound).astype(kind)


def setup_inputs(seed: int = 0) -> dict:
    key_of = jax.random.split(jax.random.key(seed), 15)
    inputs = scatter_about(key_of[0], (TOKENS, D), 1.0, 6.0, ((0, 8), (1, 4)))
    lengths = draw_lengths(jax.random.fold_in(key_of[14], 71), 0)
    norm1_gain = jnp.clip(1.0 + 0.1 * jax.random.normal(key_of[2], (D,), jnp.float32), 0.5, 1.5).astype(jnp.bfloat16)
    w_in = scatter_about(key_of[3], (D, H * (2 + 2 * HOUSE) * HEAD_DIM), D ** -0.5, 0.1875, ((0, 8), (1, 4)))
    w_small = scatter_about(key_of[4], (D, H * (HOUSE + 1)), (D // 4) ** -0.5, 0.375, ((0, 8), (1, 4)))
    conv_weight = scatter_about(key_of[5], (4, H * (1 + 2 * HOUSE) * HEAD_DIM), 4 ** -0.5, 3.0, ((1, 32),))
    decay_rate = draw_decay_rate(jax.random.fold_in(key_of[14], 71), 0)
    out_gain = jnp.clip(1.0 + 0.1 * jax.random.normal(key_of[7], (H * HEAD_DIM,), jnp.float32), 0.5, 1.5).astype(jnp.bfloat16)
    w_out = scatter_about(key_of[8], (H * HEAD_DIM, D), (H * HEAD_DIM // 4) ** -0.5, 0.375, ((0, 4), (1, 8)))
    norm2_gain = jnp.clip(1.0 + 0.1 * jax.random.normal(key_of[9], (D,), jnp.float32), 0.5, 1.5).astype(jnp.bfloat16)
    w_gate = scatter_about(key_of[10], (D, FF), D ** -0.5, 0.1875, ((0, 8), (1, 4)))
    w_up = scatter_about(key_of[11], (D, FF), D ** -0.5, 0.1875, ((0, 8), (1, 4)))
    w_down = scatter_about(key_of[12], (FF, D), (FF // 4) ** -0.5, 0.21875, ((0, 4), (1, 8)))
    cotangent = scatter_about(key_of[13], (TOKENS, D), 1.0, 6.0, ((0, 8), (1, 4)))
    return {"inputs": inputs, "lengths": lengths, "norm1_gain": norm1_gain, "w_in": w_in, "w_small": w_small, "conv_weight": conv_weight, "decay_rate": decay_rate, "out_gain": out_gain, "w_out": w_out, "norm2_gain": norm2_gain, "w_gate": w_gate, "w_up": w_up, "w_down": w_down, "cotangent": cotangent}


EPSILON = 1e-06
FULL_PRECISION = lax.Precision.HIGHEST

@jax.custom_vjp
def low(v):
    return lax.optimization_barrier(v.astype(jnp.bfloat16)).astype(jnp.float32)

@jax.custom_vjp
def low_back(v):
    return v

def low_keep(v):
    return (low(v), None)

def low_pass(kept, grad):
    return (grad,)

def back_keep(v):
    return (v, None)

def back_low(kept, grad):
    return (low(grad),)
low.defvjp(low_keep, low_pass)
low_back.defvjp(back_keep, back_low)

def product(left, right):
    return jnp.dot(left, right, precision=FULL_PRECISION)

def rms_rows(values, gain):
    return values * lax.rsqrt(lax.optimization_barrier(jnp.mean(values * values, axis=-1, keepdims=True)) + EPSILON) * gain

def document_of(positions, lengths):
    bounds = jnp.cumsum(lengths).astype(jnp.int32)
    return lax.optimization_barrier(jnp.sum((bounds[None, :] <= positions[:, None]).astype(jnp.int32), axis=1)).astype(jnp.int32)

def unit_rows(values):
    return values * lax.rsqrt(lax.optimization_barrier(jnp.sum(values * values, axis=-1, keepdims=True)) + EPSILON)

def short_conv(extended, owners, kernel):
    count = extended.shape[0] - 3
    current = owners[3:]
    total = kernel[0] * extended[3:]
    for offset in range(1, 4):
        earlier = lax.slice_in_dim(extended, 3 - offset, 3 - offset + count, axis=0)
        keep = (lax.slice_in_dim(owners, 3 - offset, 3 - offset + count, axis=0) == current).astype(jnp.float32)
        total = total + kernel[offset] * earlier * keep[:, None, None]
    return jax.nn.silu(total)

def prepare(extended, small, kernel, rate, owners):
    mixed = short_conv(extended, owners, kernel)
    rows_here, heads, channels = mixed.shape
    width = channels // (1 + 2 * HOUSE)
    queries = unit_rows(mixed[:, :, :width])
    keys = unit_rows(mixed[:, :, width:width * (1 + HOUSE)].reshape(rows_here, heads, HOUSE, width))
    values = mixed[:, :, width * (1 + HOUSE):].reshape(rows_here, heads, HOUSE, width)
    logits = small.reshape(rows_here, heads, HOUSE + 1)
    betas = 2.0 * jax.nn.sigmoid(logits[:, :, :HOUSE])
    log_decay = -rate[None, :] * jax.nn.softplus(logits[:, :, HOUSE])
    return (queries, keys, values, betas, log_decay)

def solve_lower(system, right):
    return jax.scipy.linalg.solve_triangular(system, right, lower=True, unit_diagonal=True)

def group_terms(queries, keys, values, betas, log_decay, owners, owner_before):
    rows_here, heads, house, width = keys.shape
    blocks = rows_here // GROUP
    micro = GROUP * house

    def regroup(array):
        array = array.reshape((blocks, GROUP) + array.shape[1:])
        array = jnp.swapaxes(array, 1, 2)
        return array.reshape((blocks, heads, micro) + array.shape[4:])
    key_steps = regroup(keys)
    value_steps = regroup(values)
    beta_steps = regroup(betas)
    padding = jnp.zeros((rows_here, heads, house - 1), jnp.float32)
    gate_steps = regroup(jnp.concatenate([log_decay[:, :, None], padding], axis=2))
    owner_blocks = owners.reshape(blocks, GROUP)
    owner_steps = jnp.repeat(owner_blocks, house, axis=1)
    owner_prior = jnp.concatenate([jnp.reshape(owner_before, (1,)).astype(jnp.int32), owner_blocks[:-1, -1].astype(jnp.int32)])
    query_blocks = jnp.swapaxes(queries.reshape(blocks, GROUP, heads, width), 1, 2)
    cumulative = jnp.cumsum(gate_steps, axis=-1)
    order = jnp.arange(micro)
    same = owner_steps[:, :, None] == owner_steps[:, None, :]
    reach_mask = (order[None, :] <= order[:, None])[None] & same
    spread = jnp.minimum(cumulative[..., :, None] - cumulative[..., None, :], 0.0)
    decay = jnp.where(reach_mask[:, None], jnp.exp(spread), 0.0)
    inner = jnp.einsum('bhmd,bhid->bhmi', key_steps, key_steps, precision=FULL_PRECISION)
    strict = order[None, :] < order[:, None]
    lower_part = jnp.where(strict, decay * inner * beta_steps[..., :, None], 0.0)
    system = lower_part + jnp.eye(micro, dtype=jnp.float32)
    carries = (owner_steps == owner_prior[:, None]).astype(jnp.float32)
    growth = jnp.exp(cumulative) * carries[:, None, :]
    plain_value_rows = solve_lower(system, beta_steps[..., None] * value_steps)
    state_pullback = solve_lower(system, (beta_steps * growth)[..., None] * key_steps)
    scores = decay[:, :, house - 1::house, :] * jnp.einsum('bhtd,bhid->bhti', query_blocks, key_steps, precision=FULL_PRECISION)
    query_state = growth[:, :, house - 1::house, None] * query_blocks
    carried_keys = decay[:, :, -1, :, None] * key_steps
    transfer = growth[:, :, -1, None, None] * jnp.eye(width, dtype=jnp.float32) - jnp.einsum('bhmd,bhme->bhde', carried_keys, state_pullback, precision=FULL_PRECISION)
    offset = jnp.einsum('bhmd,bhme->bhde', carried_keys, plain_value_rows, precision=FULL_PRECISION)
    return (scores, query_state, plain_value_rows, state_pullback, transfer, offset)

def run_groups(terms, state):

    def group_step(running_state_carry, piece):
        scores, query_state, plain_value_rows, state_pullback, transfer, offset = piece
        pullback_result = plain_value_rows - jnp.einsum('auq,aqb->aub', state_pullback, running_state_carry, precision=FULL_PRECISION)
        results = jnp.einsum('htd,hde->hte', query_state, running_state_carry, precision=FULL_PRECISION) + jnp.einsum('hti,hie->hte', scores, pullback_result, precision=FULL_PRECISION)
        return (jnp.einsum('hde,hef->hdf', transfer, running_state_carry, precision=FULL_PRECISION) + offset, results)
    final_state, outputs = lax.scan(group_step, state, terms)
    blocks, heads, length, width = outputs.shape
    return (jnp.swapaxes(outputs, 1, 2).reshape(blocks * length, heads, width), final_state)

def gated_output(outputs, gate_part, gain_heads):
    normed = outputs * lax.rsqrt(lax.optimization_barrier(jnp.mean(outputs * outputs, axis=-1, keepdims=True)) + EPSILON) * gain_heads
    return normed * jax.nn.silu(gate_part)

def reference(inputs, lengths, norm1_gain, w_in, w_small, conv_weight, decay_rate, out_gain, w_out, norm2_gain, w_gate, w_up, w_down, cotangent):
    weights = (norm1_gain.astype(jnp.float32), w_in.astype(jnp.float32), w_small.astype(jnp.float32), conv_weight.astype(jnp.float32), decay_rate.astype(jnp.float32), out_gain.astype(jnp.float32), w_out.astype(jnp.float32), norm2_gain.astype(jnp.float32), w_gate.astype(jnp.float32), w_up.astype(jnp.float32), w_down.astype(jnp.float32))
    starts = jnp.arange(N_SEQ, dtype=jnp.int32) * TOK_DEV
    positions = (starts[:, None] + jnp.arange(-3, TOK_DEV, dtype=jnp.int32)[None, :]).reshape(-1)
    owners_all = document_of(positions, lengths).reshape(N_SEQ, TOK_DEV + 3)

    def forward(rows_all, params):
        gain_one, proj_in, proj_small, kernel, rate, gain_out, proj_out, gain_two, gate_in, up_in, down_out = params
        kernel = kernel.reshape(4, H, -1)
        gain_heads = gain_out.reshape(H, HEAD_DIM)
        channels = kernel.shape[2]

        def block_step(carry, pieces):
            state, rim = carry
            rows, owners = pieces
            normed_one = low(rms_rows(rows, gain_one))
            projected = low_back(product(normed_one, proj_in)).reshape(TOK_DEV, H, -1)
            small = low_back(product(normed_one, proj_small))
            conv_part = projected[:, :, :channels]
            gate_part = projected[:, :, channels:]
            extended = jnp.concatenate([rim, conv_part], axis=0)
            queries, keys, values, betas, log_decay = prepare(extended, small, kernel, rate, owners)
            terms = group_terms(queries, keys, values, betas, log_decay, owners[3:], owners[2])
            outputs, new_state = run_groups(terms, state)
            gated = low(gated_output(outputs, gate_part, gain_heads).reshape(TOK_DEV, H * HEAD_DIM))
            hidden_one = rows + low_back(product(gated, proj_out))
            normed_two = low(rms_rows(hidden_one, gain_two))
            gate_pre = low_back(product(normed_two, gate_in))
            up_pre = low_back(product(normed_two, up_in))
            inner = low(jax.nn.silu(gate_pre) * up_pre)
            result = hidden_one + low_back(product(inner, down_out))
            return ((new_state, conv_part[-3:]), result)
        initial = (jnp.zeros((H, HEAD_DIM, HEAD_DIM), jnp.float32), jnp.zeros((3, H, channels), jnp.float32))
        _, results = lax.scan(jax.checkpoint(block_step), initial, (rows_all.reshape(N_SEQ, TOK_DEV, D), owners_all))
        return results.reshape(TOKENS, D)
    result, pullback = jax.vjp(forward, inputs.astype(jnp.float32), weights)
    grad_rows, grad_params = pullback(cotangent.astype(jnp.float32))
    return (result.astype(jnp.bfloat16), grad_rows, grad_params[0], grad_params[1], grad_params[2], grad_params[3], grad_params[4], grad_params[5], grad_params[6], grad_params[7], grad_params[8], grad_params[9], grad_params[10])
```

```python
from functools import partial

import jax
import jax.numpy as jnp
from jax import lax
from jax.experimental import pallas as pl
from jax.experimental.pallas import tpu as pltpu
from jax.sharding import PartitionSpec as P

HOUSE = 2
GROUP = 64
MICRO = GROUP * HOUSE
WIDTH = 128
RIM = 16
EPSILON = 1e-06
MESH = pl.DeviceIdType.MESH
VMEM_BYTES = 56 * 2**20
F32 = jnp.float32
BF16 = jnp.bfloat16

VMEM = pl.BlockSpec(memory_space=pltpu.VMEM)
SMEM = pl.BlockSpec(memory_space=pltpu.SMEM)
ANY = pl.BlockSpec(memory_space=pl.ANY)
DMA = pltpu.SemaphoreType.DMA


def shape(dims, kind):
    return jax.ShapeDtypeStruct(tuple(dims), kind)


def dot(left, right, over=(1, 0)):
    return lax.dot_general(
        left, right, (((over[0],), (over[1],)), ((), ())), preferred_element_type=F32
    )


def dot_low(left, right, over=(1, 0)):
    return dot(left.astype(BF16), right.astype(BF16), over)


def halves(values):
    high = values.astype(BF16)
    return high, (values - high.astype(F32)).astype(BF16)


def dot_mid(left, right, over=(1, 0)):
    left_high, left_low = halves(left)
    right_high, right_low = halves(right)
    return (
        dot(left_high, right_low, over)
        + dot(left_low, right_high, over)
        + dot(left_high, right_high, over)
    )


def rows_of(count):
    return lax.broadcasted_iota(jnp.int32, (count, 1), 0)


def lanes_of(count):
    return lax.broadcasted_iota(jnp.int32, (1, count), 1)


def to_lane(column):
    count = column.shape[0]
    return jnp.sum(jnp.where(rows_of(count) == lanes_of(count), column, 0.0), axis=0, keepdims=True)


def to_column(lane):
    count = lane.shape[1]
    return jnp.sum(jnp.where(rows_of(count) == lanes_of(count), lane, 0.0), axis=1, keepdims=True)


def row_sum(values):
    return jnp.sum(values, axis=1, keepdims=True)


def bounds_of(lengths_ref):
    bounds = []
    total = 0
    for at in range(lengths_ref.shape[0]):
        total = total + lengths_ref[at]
        bounds.append(total)
    return bounds


def owner_of(positions, bounds):
    total = jnp.zeros_like(positions)
    for bound in bounds:
        total = total + (bound <= positions).astype(jnp.int32)
    return total


def micro_order(index):
    return 2 * (index & (GROUP - 1)) + lax.shift_right_logical(index, 6)


def unit_inverse(lowers):
    above, left = micro_order(rows_of(MICRO)), micro_order(lanes_of(MICRO))
    eye = (rows_of(MICRO) == lanes_of(MICRO)).astype(F32)

    def level_mask(level):
        step = 1 << level
        return (
            (lax.shift_right_logical(above, level + 1) == lax.shift_right_logical(left, level + 1))
            & ((above & step) != 0)
            & ((left & step) == 0)
        )

    first = level_mask(0)
    found = [eye - jnp.where(first, lower, 0.0) for lower in lowers]
    for level in range(1, 7):
        mask = level_mask(level)
        inner = [dot_mid(jnp.where(mask, a, 0.0), b) for a, b in zip(lowers, found)]
        found = [b - dot_mid(b, a) for a, b in zip(inner, found)]
    return found


def conv_window(proj_ref, group, column):
    start = pl.multiple_of(group * GROUP + RIM - 8, 8)
    window = proj_ref[pl.ds(start, GROUP + 8), column : column + WIDTH]
    return [window[8 - step : GROUP + 8 - step] for step in range(4)]


def conv_keeps(group, first, bounds):
    positions = first + group * GROUP + rows_of(GROUP)
    current = owner_of(positions, bounds)
    return [None] + [
        (owner_of(positions - step, bounds) == current).astype(F32) for step in range(1, 4)
    ]


def conv_total(parts, keeps, taps_ref, column):
    total = parts[0] * taps_ref[0:1, column : column + WIDTH]
    for step in range(1, 4):
        total = total + parts[step] * keeps[step] * taps_ref[step : step + 1, column : column + WIDTH]
    return total


def gate_terms(small_ref, rate, group, head):
    logits = small_ref[pl.ds(pl.multiple_of(group * GROUP, GROUP), GROUP), :]
    at = head * (HOUSE + 1)
    betas = 2.0 * jax.nn.sigmoid(logits[:, at : at + HOUSE])
    decay_logit = logits[:, at + HOUSE : at + HOUSE + 1]
    soft = jnp.maximum(decay_logit, 0.0) + jnp.log(1.0 + jnp.exp(-jnp.abs(decay_logit)))
    log_decay = -rate * soft
    upto = lanes_of(GROUP) <= rows_of(GROUP)
    cumulative = row_sum(jnp.where(upto, to_lane(log_decay), 0.0))
    return betas, decay_logit, soft, cumulative


def group_masks(group, first, bounds):
    order, order_lane = micro_order(rows_of(MICRO)), micro_order(lanes_of(MICRO))
    start = first + group * GROUP
    owners = owner_of(start + (rows_of(MICRO) & (GROUP - 1)), bounds)
    owners_lane = owner_of(start + (lanes_of(MICRO) & (GROUP - 1)), bounds)
    prior = owner_of(jnp.full((1, 1), start - 1, jnp.int32), bounds)
    last = owner_of(jnp.full((1, 1), start + GROUP - 1, jnp.int32), bounds)
    same = owners == owners_lane
    reach = same & (order_lane <= order)
    strict = order_lane < order
    carries = (owners == prior).astype(F32)
    ends = owners == last
    return reach, strict, carries, ends


def decay_terms(cumulative, masks):
    reach, strict, carries, ends = masks
    column = jnp.concatenate([cumulative, cumulative], axis=0)
    lane = to_lane(column)
    decay = jnp.where(reach, jnp.exp(jnp.minimum(column - lane, 0.0)), 0.0)
    growth = jnp.exp(column) * carries
    final = column[MICRO - 1 : MICRO]
    to_end = jnp.where(ends, jnp.exp(jnp.minimum(final - column, 0.0)), 0.0)
    return decay, growth, to_end


def seq_links():
    me_seq, me_head = lax.axis_index("seq"), lax.axis_index("head")
    outer = lax.axis_size("seq") // 2
    place, inner = me_seq // 2, lax.rem(me_seq, 2)
    return me_seq, me_head, outer, place, inner


def other_of(index):
    return index + 1 - 2 * lax.rem(index, 2)


def greet(devices):
    barrier = pltpu.get_barrier_semaphore()
    count = 0
    for condition, device in devices:
        if condition is None:
            pl.semaphore_signal(barrier, inc=1, device_id=device, device_id_type=MESH)
            count = count + 1
        else:

            @pl.when(condition)
            def _():
                pl.semaphore_signal(barrier, inc=1, device_id=device, device_id_type=MESH)

            count = count + jnp.where(condition, 1, 0)
    pl.semaphore_wait(barrier, count)


def seq_neighbours():
    me_seq, me_head, outer, place, inner = seq_links()
    return [
        (None, (other_of(me_seq), me_head)),
        (place < outer - 1, (me_seq + 2, me_head)),
        (place > 0, (me_seq - 2, me_head)),
    ]


def head_neighbours():
    me_seq, me_head = lax.axis_index("seq"), lax.axis_index("head")
    outer = lax.axis_size("head") // 2
    found = [(None, (me_seq, other_of(me_head)))]
    for step in range(1, outer):
        found.append((None, (me_seq, lax.rem(me_head + 2 * step, 2 * outer))))
    return found


def remote(source, target, send, receive, device):
    return pltpu.make_async_remote_copy(
        src_ref=source,
        dst_ref=target,
        send_sem=send,
        recv_sem=receive,
        device_id=device,
        device_id_type=MESH,
    )


class SeqGather:
    def __init__(self, source, target, sends, receives):
        self.source, self.target = source, target
        self.sends, self.receives = sends, receives

    def block(self, origin):
        return self.target.at[origin]

    def send(self, origin, way, device, source=None):
        source = self.block(origin) if source is None else source
        remote(
            source, self.block(origin), self.sends.at[origin, way], self.receives.at[origin], device
        ).start()

    def wait_send(self, origin, way):
        me_seq, me_head, outer, place, inner = seq_links()
        remote(
            self.block(origin),
            self.block(origin),
            self.sends.at[origin, way],
            self.receives.at[origin],
            (me_seq, me_head),
        ).wait_send()

    def wait_arrival(self, origin):
        me_seq, me_head, outer, place, inner = seq_links()
        remote(
            self.block(origin),
            self.block(origin),
            self.sends.at[origin, 0],
            self.receives.at[origin],
            (me_seq, me_head),
        ).wait_recv()

    def start(self, local):
        me_seq, me_head, outer, place, inner = seq_links()
        self.local = pltpu.make_async_copy(self.source, self.block(me_seq), local)
        self.local.start()

        @pl.when(place < outer - 1)
        def _():
            self.send(me_seq, 0, (me_seq + 2, me_head), self.source)

        @pl.when(place > 0)
        def _():
            self.send(me_seq, 1, (me_seq - 2, me_head), self.source)

        self.send(me_seq, 2, (other_of(me_seq), me_head), self.source)

    def relay(self, step):
        me_seq, me_head, outer, place, inner = seq_links()
        below, above = me_seq - 2 * step, me_seq + 2 * step
        aside = (other_of(me_seq), me_head)

        @pl.when(place >= step)
        def _():
            self.wait_arrival(below)

            @pl.when(place < outer - 1)
            def _():
                self.send(below, 0, (me_seq + 2, me_head))

            self.send(below, 2, aside)

        @pl.when(place < outer - step)
        def _():
            self.wait_arrival(above)

            @pl.when(place > 0)
            def _():
                self.send(above, 1, (me_seq - 2, me_head))

            self.send(above, 2, aside)

    def finish(self):
        me_seq, me_head, outer, place, inner = seq_links()
        self.local.wait()
        for at in range(outer):
            self.wait_arrival(2 * at + 1 - inner)
        for at in range(outer):
            origin = 2 * at + inner
            self.wait_send(origin, 2)

            @pl.when((at <= place) & (place < outer - 1))
            def _():
                self.wait_send(origin, 0)

            @pl.when((at >= place) & (place > 0))
            def _():
                self.wait_send(origin, 1)


class HeadGather:
    def __init__(self, source, place_of, sends, receives):
        self.source, self.place_of = source, place_of
        self.sends, self.receives = sends, receives

    def links(self):
        me_seq, me_head = lax.axis_index("seq"), lax.axis_index("head")
        return me_seq, me_head, lax.axis_size("head") // 2

    def copy(self, origin, way, device, source=None):
        target = self.place_of(origin)
        return remote(
            target if source is None else source,
            target,
            self.sends.at[origin, way],
            self.receives.at[origin],
            device,
        )

    def start(self, local=None):
        me_seq, me_head, outer = self.links()
        self.local = None
        if local is not None:
            self.local = pltpu.make_async_copy(self.source, self.place_of(me_head), local)
            self.local.start()
        for step in range(1, outer):
            device = (me_seq, lax.rem(me_head + 2 * step, 2 * outer))
            self.copy(me_head, step, device, self.source).start()
        self.copy(me_head, 0, (me_seq, other_of(me_head)), self.source).start()

    def hand_on(self):
        me_seq, me_head, outer = self.links()
        for step in range(1, outer):
            origin = lax.rem(me_head + 2 * (outer - step), 2 * outer)
            self.copy(origin, 0, (me_seq, me_head)).wait_recv()
            self.copy(origin, 0, (me_seq, other_of(me_head))).start()

    def finish(self):
        me_seq, me_head, outer = self.links()
        if self.local is not None:
            self.local.wait()
        for step in range(outer):
            origin = lax.rem(other_of(me_head) + 2 * step, 2 * outer)
            self.copy(origin, 0, (me_seq, me_head)).wait_recv()
        for step in range(outer):
            origin = lax.rem(me_head + 2 * step, 2 * outer)
            self.copy(origin, 0, (me_seq, me_head)).wait_send()
        for step in range(1, outer):
            self.copy(me_head, step, (me_seq, me_head)).wait_send()


def entry_kernel(seq_count, wide_count, *refs):
    refs = list(refs)
    take = lambda count: [refs.pop(0) for _ in range(count)]
    columns, cotangent = take(2)
    shards = take(seq_count)
    rows, grad_rows, rim = take(3)
    gathered = take(seq_count)
    wide = take(wide_count)
    head_sends, head_receives, local, rim_send, rim_receive = take(5)
    seq_sends, seq_receives = take(2)
    wide_sends, wide_receives = take(2)
    me_seq, me_head, outer, place, inner = seq_links()
    count = lax.axis_size("seq")
    after = (lax.rem(me_seq + 1, count), me_head)
    before = (lax.rem(me_seq + count - 1, count), me_head)
    greet(seq_neighbours() + head_neighbours() + [(None, after), (None, before)])
    span = columns.shape[1]

    def part_of(target):
        return lambda origin: target.at[:, pl.ds(pl.multiple_of(origin * span, span), span)]

    heads = [
        HeadGather(columns, part_of(rows), head_sends.at[0], head_receives.at[0]),
        HeadGather(cotangent, part_of(grad_rows), head_sends.at[1], head_receives.at[1]),
    ]
    gathers = [
        SeqGather(shard, target, seq_sends.at[at], seq_receives.at[at])
        for at, (shard, target) in enumerate(zip(shards, gathered))
    ]
    heads[0].start(local.at[0])
    for at, gather in enumerate(gathers):
        gather.start(local.at[2 + at])
    heads[1].start(local.at[1])
    heads[0].hand_on()
    heads[0].finish()
    tail = rows.at[pl.ds(rows.shape[0] - RIM, RIM), :]
    rim_copy = remote(tail, rim, rim_send, rim_receive, after)
    rim_copy.start()
    heads[1].hand_on()
    for step in range(1, outer):
        for gather in gathers:
            gather.relay(step)
    for gather in gathers:
        gather.finish()
    heads[1].finish()
    rim_copy.wait()
    spread = [
        HeadGather(
            gathered[at],
            (lambda origin, target=target: target.at[origin]),
            wide_sends.at[at],
            wide_receives.at[at],
        )
        for at, target in enumerate(wide)
    ]
    for at, gather in enumerate(spread):
        gather.start(local.at[2 + at])
    for gather in spread:
        gather.hand_on()
    for gather in spread:
        gather.finish()


def entry(columns, cotangent, shards, wide_count, n_seq, n_head):
    rows_here, span = columns.shape
    full = (rows_here, span * n_head)
    gathered = [shape((n_seq,) + a.shape, a.dtype) for a in shards]
    wide = [shape((n_head, n_seq) + a.shape, a.dtype) for a in shards[:wide_count]]
    count = len(shards)
    outs = pl.pallas_call(
        partial(entry_kernel, count, wide_count),
        out_shape=[shape(full, BF16), shape(full, BF16), shape((RIM, full[1]), BF16)]
        + gathered
        + wide,
        in_specs=[ANY] * (2 + count),
        out_specs=[ANY] * (3 + count + wide_count),
        scratch_shapes=[
            DMA((2, n_head, n_head // 2)),
            DMA((2, n_head)),
            DMA((2 + count,)),
            DMA,
            DMA,
            DMA((count, n_seq, 3)),
            DMA((count, n_seq)),
            DMA((wide_count, n_head, n_head // 2)),
            DMA((wide_count, n_head)),
        ],
        compiler_params=pltpu.CompilerParams(
            collective_id=0, has_side_effects=True, vmem_limit_bytes=VMEM_BYTES
        ),
        name="entry_gathers",
    )(columns, cotangent, *shards)
    return outs[0], outs[1], outs[2], outs[3 : 3 + count], outs[3 + count :]


def mixer_kernel(
    lengths_ref,
    rate_ref,
    rows_ref,
    rim_ref,
    gain_ref,
    w_in_ref,
    w_small_ref,
    taps_ref,
    normed_ref,
    proj_ref,
    small_ref,
    query_ref,
    key_ref,
    value_ref,
    inverse_ref,
    solved_ref,
    lower_ref,
    scores_ref,
    reach_ref,
    local_ref,
    map_ref,
    add_ref,
    before_ref,
    total_ref,
):
    rows_here, model = rows_ref.shape
    heads, groups = key_ref.shape[:2]
    block = proj_ref.shape[1] // heads
    me_seq = lax.axis_index("seq")
    first = me_seq * rows_here
    bounds = bounds_of(lengths_ref)

    def normed_of(values):
        values = values.astype(F32)
        scale = lax.rsqrt(row_sum(values * values) / model + EPSILON)
        return (values * scale * gain_ref[...]).astype(BF16)

    rim = jnp.where(me_seq > 0, rim_ref[...].astype(F32), 0.0)
    normed_ref[0:RIM, :] = normed_of(rim)
    proj_ref[0:RIM, :] = dot(normed_ref[0:RIM, :], w_in_ref[...])
    tile = min(128, rows_here)

    @pl.loop(0, rows_here // tile)
    def _(at):
        start = pl.multiple_of(at * tile, tile)
        normed = normed_of(rows_ref[pl.ds(start, tile), :])
        shifted = pl.multiple_of(start + RIM, RIM)
        normed_ref[pl.ds(shifted, tile), :] = normed
        proj_ref[pl.ds(shifted, tile), :] = dot(normed, w_in_ref[...])
        small_ref[pl.ds(start, tile), :] = dot(normed, w_small_ref[...])

    eye = (rows_of(MICRO) == lanes_of(MICRO)).astype(F32)
    together = 2

    @pl.loop(0, groups // together)
    def _(pair):
        units = []
        for extra in range(together):
            group = pair * together + extra
            keeps = conv_keeps(group, first, bounds)
            masks = group_masks(group, first, bounds)
            for head in range(heads):
                blocks = []
                for part in range(1 + 2 * HOUSE):
                    parts = conv_window(proj_ref, group, head * block + part * WIDTH)
                    taps = head * (1 + 2 * HOUSE) * WIDTH + part * WIDTH
                    total = conv_total(parts, keeps, taps_ref, taps)
                    mixed = total * jax.nn.sigmoid(total)
                    if part < 1 + HOUSE:
                        mixed = mixed * lax.rsqrt(row_sum(mixed * mixed) + EPSILON)
                    blocks.append(mixed)
                query = blocks[0]
                keys = jnp.concatenate(blocks[1 : 1 + HOUSE], axis=0)
                values = jnp.concatenate(blocks[1 + HOUSE :], axis=0)
                betas, _, _, cumulative = gate_terms(small_ref, rate_ref[head], group, head)
                beta = jnp.concatenate([betas[:, 0:1], betas[:, 1:2]], axis=0)
                decay, growth, to_end = decay_terms(cumulative, masks)
                inner = dot_mid(keys, keys, (1, 1))
                lower = jnp.where(masks[1], decay * inner * beta, 0.0)
                query_ref[head, group] = query
                key_ref[head, group] = keys
                value_ref[head, group] = values
                lower_ref[head, group] = lower
                units.append((head, group, query, keys, values, beta, decay, growth, to_end, lower))
        inverses = unit_inverse([unit[-1] for unit in units])
        for unit, inverse in zip(units, inverses):
            head, group, query, keys, values, beta, decay, growth, to_end, lower = unit
            right = jnp.concatenate([beta * values, (beta * growth) * keys], axis=1)
            solved = dot_mid(inverse, right)
            scores = decay[GROUP:] * dot_mid(query, keys, (1, 1))
            seen = dot_mid(scores, solved)
            carried = dot_mid(to_end * keys, solved, (0, 0))
            inverse_ref[head, group] = inverse
            solved_ref[head, group] = solved
            scores_ref[head, group] = scores
            local_ref[head, group] = seen[:, :WIDTH]
            reach_ref[head, group] = growth[GROUP:] * query - seen[:, WIDTH:]
            map_ref[head, group] = growth[MICRO - 1 : MICRO] * eye - carried[:, WIDTH:]
            add_ref[head, group] = carried[:, :WIDTH]

    for head in range(heads):
        total_ref[head] = jnp.concatenate([eye, jnp.zeros((WIDTH, WIDTH), F32)], axis=1)

    @pl.loop(0, groups)
    def _(group):
        for head in range(heads):
            so_far = total_ref[head]
            before_ref[head, group] = so_far
            joined = dot_mid(map_ref[head, group], so_far)
            added = jnp.concatenate([jnp.zeros((WIDTH, WIDTH), F32), add_ref[head, group]], axis=1)
            total_ref[head] = joined + added


def mixer(lengths, rate, rows, rim, gain, w_in, w_small, taps):
    rows_here, model = rows.shape
    heads = rate.shape[0]
    groups = rows_here // GROUP
    unit = (heads, groups)
    return pl.pallas_call(
        mixer_kernel,
        out_shape=[
            shape((rows_here + RIM, model), BF16),
            shape((rows_here + RIM, w_in.shape[1]), F32),
            shape((rows_here, WIDTH), F32),
            shape(unit + (GROUP, WIDTH), F32),
            shape(unit + (MICRO, WIDTH), F32),
            shape(unit + (MICRO, WIDTH), F32),
            shape(unit + (MICRO, MICRO), F32),
            shape(unit + (MICRO, 2 * WIDTH), F32),
            shape(unit + (MICRO, MICRO), F32),
            shape(unit + (GROUP, MICRO), F32),
            shape(unit + (GROUP, WIDTH), F32),
            shape(unit + (GROUP, WIDTH), F32),
            shape(unit + (WIDTH, WIDTH), F32),
            shape(unit + (WIDTH, WIDTH), F32),
            shape(unit + (WIDTH, 2 * WIDTH), F32),
            shape((heads, WIDTH, 2 * WIDTH), F32),
        ],
        in_specs=[SMEM, SMEM] + [VMEM] * 6,
        out_specs=[VMEM] * 16,
        compiler_params=pltpu.CompilerParams(vmem_limit_bytes=VMEM_BYTES),
        name="mixer_terms",
    )(lengths, rate, rows, rim, gain, w_in, w_small, taps)


def state_kernel(total_ref, state_ref, pair_ref, aside_ref, own, theirs, moving, arriving, sems):
    me_seq, me_head, outer, place, inner = seq_links()
    heads = total_ref.shape[0]
    greet(seq_neighbours())
    own[...] = total_ref[...].astype(BF16)
    swap = remote(own, theirs, sems.at[0], sems.at[1], (other_of(me_seq), me_head))
    swap.start()
    swap.wait()
    for head in range(heads):
        mine, other = own[head].astype(F32), theirs[head].astype(F32)
        aside_ref[head] = other
        early = jnp.where(inner == 0, mine, other)
        late = jnp.where(inner == 0, other, mine)
        joined = dot_mid(late[:, :WIDTH], early)
        zero = jnp.zeros((WIDTH, WIDTH), F32)
        pair_ref[head] = joined + jnp.concatenate([zero, late[:, WIDTH:]], axis=1)

    step_up = remote(moving, arriving, sems.at[2], sems.at[3], (me_seq + 2, me_head))

    @pl.when(place > 0)
    def _():
        step_up.wait_recv()

    for head in range(heads):
        state = jnp.where(place > 0, arriving[head].astype(F32), 0.0)
        moved = dot_mid(pair_ref[head, :, :WIDTH], state) + pair_ref[head, :, WIDTH:]
        moving[head] = moved.astype(BF16)

    @pl.when(place < outer - 1)
    def _():
        step_up.start()

    for head in range(heads):
        state = jnp.where(place > 0, arriving[head].astype(F32), 0.0)
        stepped = dot_mid(aside_ref[head, :, :WIDTH], state) + aside_ref[head, :, WIDTH:]
        state_ref[head] = jnp.where(inner == 0, state, stepped)

    @pl.when(place < outer - 1)
    def _():
        step_up.wait_send()


def carry_state(total):
    heads = total.shape[0]
    square = (heads, WIDTH, WIDTH)
    both = (heads, WIDTH, 2 * WIDTH)
    return pl.pallas_call(
        state_kernel,
        out_shape=[shape(square, F32), shape(both, F32), shape(both, F32)],
        in_specs=[VMEM],
        out_specs=[VMEM] * 3,
        scratch_shapes=[
            pltpu.VMEM(both, BF16),
            pltpu.VMEM(both, BF16),
            pltpu.VMEM(square, BF16),
            pltpu.VMEM(square, BF16),
            DMA((4,)),
        ],
        compiler_params=pltpu.CompilerParams(
            collective_id=1, has_side_effects=True, vmem_limit_bytes=VMEM_BYTES
        ),
        name="state_relay",
    )(total)


def adjoint_kernel(
    residual_ref, pair_ref, aside_ref, adjoint_ref, own, theirs, moving, arriving, sems
):
    me_seq, me_head, outer, place, inner = seq_links()
    heads = residual_ref.shape[0]
    greet(seq_neighbours())
    own[...] = residual_ref[...].astype(BF16)
    swap = remote(own, theirs, sems.at[0], sems.at[1], (other_of(me_seq), me_head))
    swap.start()
    swap.wait()
    step_down = remote(moving, arriving, sems.at[2], sems.at[3], (me_seq - 2, me_head))

    @pl.when(place < outer - 1)
    def _():
        step_down.wait_recv()

    for head in range(heads):
        mine, other = own[head].astype(F32), theirs[head].astype(F32)
        adjoint = jnp.where(place < outer - 1, arriving[head].astype(F32), 0.0)
        late_after = jnp.where(inner == 0, other, mine)
        early_after = jnp.where(inner == 0, mine, other)
        map_other = aside_ref[head, :, :WIDTH]
        stepped = late_after + dot_mid(map_other, adjoint, (0, 0))
        adjoint_ref[head] = jnp.where(inner == 0, stepped, adjoint)
        pair_map = pair_ref[head, :, :WIDTH]
        early_map = jnp.where(inner == 0, pair_ref[head, :, WIDTH:], map_other)
        joined = early_after + dot_mid(early_map, late_after, (0, 0))
        moving[head] = (joined + dot_mid(pair_map, adjoint, (0, 0))).astype(BF16)

    @pl.when(place > 0)
    def _():
        step_down.start()
        step_down.wait_send()


def carry_adjoint(residual, pair, aside):
    heads = residual.shape[0]
    square = (heads, WIDTH, WIDTH)
    return pl.pallas_call(
        adjoint_kernel,
        out_shape=shape(square, F32),
        in_specs=[VMEM] * 3,
        out_specs=VMEM,
        scratch_shapes=[pltpu.VMEM(square, BF16)] * 4 + [DMA((4,))],
        compiler_params=pltpu.CompilerParams(
            collective_id=2, has_side_effects=True, vmem_limit_bytes=VMEM_BYTES
        ),
        name="adjoint_relay",
    )(residual, pair, aside)


def gated_kernel(
    state_ref, before_ref, local_ref, reach_ref, proj_ref, gain_ref, gated_ref, starts_ref, out_ref
):
    heads, groups = before_ref.shape[:2]
    block = proj_ref.shape[1] // heads

    @pl.loop(0, groups)
    def _(group):
        rows = pl.ds(pl.multiple_of(group * GROUP, GROUP), GROUP)
        shifted = pl.ds(pl.multiple_of(group * GROUP + RIM, RIM), GROUP)
        for head in range(heads):
            before = before_ref[head, group]
            start = dot_mid(before[:, :WIDTH], state_ref[head]) + before[:, WIDTH:]
            starts_ref[head, group] = start
            out = local_ref[head, group] + dot_mid(reach_ref[head, group], start)
            span = slice(head * WIDTH, (head + 1) * WIDTH)
            out_ref[rows, span] = out
            scale = lax.rsqrt(row_sum(out * out) / WIDTH + EPSILON)
            gate = proj_ref[shifted, (head + 1) * block - WIDTH : (head + 1) * block]
            gated = out * scale * gain_ref[:, span] * (gate * jax.nn.sigmoid(gate))
            gated_ref[rows, span] = gated.astype(BF16)


def gated_output(state, before, local, reach, proj, gain, rows_here):
    heads, groups = before.shape[:2]
    return pl.pallas_call(
        gated_kernel,
        out_shape=[
            shape((rows_here, heads * WIDTH), BF16),
            shape((heads, groups, WIDTH, WIDTH), F32),
            shape((rows_here, heads * WIDTH), F32),
        ],
        in_specs=[VMEM] * 6,
        out_specs=[VMEM] * 3,
        compiler_params=pltpu.CompilerParams(vmem_limit_bytes=VMEM_BYTES),
        name="mixer_output",
    )(state, before, local, reach, proj, gain)


def gather_rows_kernel(source, rows, sends, receives, local):
    greet(head_neighbours())
    span = source.shape[1]
    gather = HeadGather(
        source,
        lambda origin: rows.at[:, pl.ds(pl.multiple_of(origin * span, span), span)],
        sends,
        receives,
    )
    gather.start(local)
    gather.hand_on()
    gather.finish()


def gather_rows(values, n_head):
    return pl.pallas_call(
        gather_rows_kernel,
        out_shape=shape((values.shape[0], values.shape[1] * n_head), values.dtype),
        in_specs=[ANY],
        out_specs=ANY,
        scratch_shapes=[DMA((n_head, n_head // 2)), DMA((n_head,)), DMA],
        compiler_params=pltpu.CompilerParams(
            collective_id=3, has_side_effects=True, vmem_limit_bytes=VMEM_BYTES
        ),
        name="gather_gated",
    )(values)


def forward_kernel(
    rows_ref,
    gated_ref,
    w_out_ref,
    gain_ref,
    gate_ref,
    up_ref,
    down_ref,
    grad_ref,
    hidden_ref,
    normed_ref,
    inner_ref,
    out_ref,
    grad_gate_ref,
    grad_up_ref,
    grad_normed_ref,
):
    rows_here, model = rows_ref.shape
    heads, _, span = w_out_ref.shape
    tile = min(256, rows_here)

    @pl.loop(0, rows_here // tile)
    def _(at):
        rows = pl.ds(pl.multiple_of(at * tile, tile), tile)
        hidden = rows_ref[rows, :].astype(F32)
        for head in range(heads):
            part = gated_ref[rows, head * span : (head + 1) * span]
            hidden = hidden + dot(part, w_out_ref[head], (1, 1))
        hidden_ref[rows, :] = hidden
        scale = lax.rsqrt(row_sum(hidden * hidden) / model + EPSILON)
        normed = (hidden * scale * gain_ref[...]).astype(BF16)
        normed_ref[rows, :] = normed
        gate = dot(normed, gate_ref[...])
        up = dot(normed, up_ref[...])
        sigma = jax.nn.sigmoid(gate)
        swish = gate * sigma
        inner = (swish * up).astype(BF16)
        inner_ref[rows, :] = inner
        out_ref[rows, :] = dot(inner, down_ref[...], (1, 1)).astype(BF16)
        grad_inner = dot(grad_ref[rows, :], down_ref[...])
        grad_gate = (grad_inner * up * sigma * (1.0 + gate * (1.0 - sigma))).astype(BF16)
        grad_up = (grad_inner * swish).astype(BF16)
        grad_gate_ref[rows, :] = grad_gate
        grad_up_ref[rows, :] = grad_up
        back = dot(grad_gate, gate_ref[...], (1, 1)) + dot(grad_up, up_ref[...], (1, 1))
        grad_normed_ref[rows, :] = back.astype(BF16)


def feed_forward(rows, gated, w_out, gain, gate_in, up_in, down, grad_rows):
    rows_here, model = rows.shape
    units = gate_in.shape[1]
    return pl.pallas_call(
        forward_kernel,
        out_shape=[
            shape((rows_here, model), F32),
            shape((rows_here, model), BF16),
            shape((rows_here, units), BF16),
            shape((rows_here, model), BF16),
            shape((rows_here, units), BF16),
            shape((rows_here, units), BF16),
            shape((rows_here, model), BF16),
        ],
        in_specs=[VMEM] * 8,
        out_specs=[VMEM] * 7,
        compiler_params=pltpu.CompilerParams(vmem_limit_bytes=VMEM_BYTES),
        name="feed_forward",
    )(rows, gated, w_out, gain, gate_in, up_in, down, grad_rows)


class HeadSum:
    def __init__(self, source, cores, chips, sends, receives):
        self.source, self.cores, self.chips = source, cores, chips
        self.sends, self.receives = sends, receives
        self.span = source.shape[1] // lax.axis_size("head")

    def links(self):
        me_seq, me_head = lax.axis_index("seq"), lax.axis_index("head")
        return me_seq, me_head, lax.axis_size("head") // 2

    def columns(self, origin):
        return pl.ds(pl.multiple_of(origin * self.span, self.span), self.span)

    def to_core(self, at):
        me_seq, me_head, outer = self.links()
        far = 2 * at + 1 - lax.rem(me_head, 2)
        return remote(
            self.source.at[:, self.columns(far)],
            self.cores.at[at],
            self.sends.at[at],
            self.receives.at[at],
            (me_seq, other_of(me_head)),
        )

    def start(self):
        for at in range(self.links()[2]):
            self.to_core(at).start()

    def add_core(self, at):
        me_seq, me_head, outer = self.links()
        self.to_core(at).wait()
        near = 2 * at + lax.rem(me_head, 2)
        tile = min(128, self.source.shape[0])

        @pl.loop(0, self.source.shape[0] // tile)
        def _(turn):
            rows = pl.ds(pl.multiple_of(turn * tile, tile), tile)
            total = self.source[rows, self.columns(near)].astype(F32) + self.cores[at, rows, :].astype(F32)
            self.cores[at, rows, :] = total.astype(BF16)


def norm_kernel(
    partial_ref,
    out_ref,
    hidden_ref,
    grad_ref,
    gain_ref,
    result_ref,
    grad_hidden_ref,
    branch_ref,
    grad_gain_ref,
    total,
    cores,
    chips,
    out_cores,
    out_chips,
    sends,
    receives,
    chip_sends,
    chip_receives,
    last_sends,
    last_receives,
):
    rows_here, model = partial_ref.shape
    me_seq, me_head = lax.axis_index("seq"), lax.axis_index("head")
    outer = lax.axis_size("head") // 2
    chip, core = me_head // 2, lax.rem(me_head, 2)
    span = model // (2 * outer)
    greet(head_neighbours())
    back = HeadSum(partial_ref, cores, chips, sends.at[0], receives.at[0])
    ahead = HeadSum(out_ref, out_cores, out_chips, sends.at[1], receives.at[1])
    back.start()
    ahead.start()

    def columns(origin):
        return pl.ds(pl.multiple_of(origin * span, span), span)

    def to_chip(step):
        return remote(
            cores,
            chips.at[step],
            chip_sends.at[0, step],
            chip_receives.at[0, step],
            (me_seq, lax.rem(me_head + 2 * step, 2 * outer)),
        )

    def out_to_chip(step):
        target = lax.rem(me_head + 2 * step, 2 * outer)
        return remote(
            out_cores.at[target // 2],
            out_chips.at[step],
            chip_sends.at[1, step],
            chip_receives.at[1, step],
            (me_seq, target),
        )

    for at in range(outer):
        back.add_core(at)
    for step in range(1, outer):
        to_chip(step).start()
    for at in range(outer):
        ahead.add_core(at)
    for step in range(1, outer):
        out_to_chip(step).start()
    for step in range(1, outer):
        to_chip(step).wait()
    tile = min(128, rows_here)

    def to_total(at):
        far = columns(2 * at + core)
        return remote(
            total.at[:, far],
            total.at[:, far],
            last_sends.at[at],
            last_receives.at[at],
            (me_seq, other_of(me_head)),
        )

    for at in range(outer):

        @pl.loop(0, rows_here // tile)
        def _(turn):
            rows = pl.ds(pl.multiple_of(turn * tile, tile), tile)
            value = cores[at, rows, :].astype(F32)
            for step in range(1, outer):
                value = value + chips[step, at, rows, :].astype(F32)
            total[rows, columns(2 * at + core)] = value.astype(BF16)

        to_total(at).start()
    for at in range(outer):
        to_total(at).wait()

    own = columns(me_head)
    grad_gain_ref[...] = jnp.zeros_like(grad_gain_ref)

    @pl.loop(0, rows_here // tile)
    def _(turn):
        rows = pl.ds(pl.multiple_of(turn * tile, tile), tile)
        hidden = hidden_ref[rows, :]
        scale = lax.rsqrt(row_sum(hidden * hidden) / model + EPSILON)
        weighted = total[rows, :].astype(F32) * gain_ref[...]
        inner = row_sum(weighted * hidden)
        grad = scale * weighted - hidden * (scale * scale * scale * inner / model)
        grad = grad + grad_ref[rows, :].astype(F32)
        branch_ref[rows, :] = grad.astype(BF16)

    @pl.loop(0, rows_here // tile)
    def _(turn):
        rows = pl.ds(pl.multiple_of(turn * tile, tile), tile)
        whole = hidden_ref[rows, :]
        scale = lax.rsqrt(row_sum(whole * whole) / model + EPSILON)
        weighted = total[rows, :].astype(F32) * gain_ref[...]
        inner = row_sum(weighted * whole)
        hidden = hidden_ref[rows, own]
        back_rows = total[rows, own].astype(F32)
        grad = scale * back_rows * gain_ref[:, own] - hidden * (scale * scale * scale * inner / model)
        grad_hidden_ref[rows, :] = grad + grad_ref[rows, own].astype(F32)
        grad_gain_ref[...] += jnp.sum(back_rows * hidden * scale, axis=0, keepdims=True)

    for step in range(1, outer):
        out_to_chip(step).wait()

    @pl.loop(0, rows_here // tile)
    def _(turn):
        rows = pl.ds(pl.multiple_of(turn * tile, tile), tile)
        value = hidden_ref[rows, own] + out_cores[chip, rows, :].astype(F32)
        for step in range(1, outer):
            value = value + out_chips[step, rows, :].astype(F32)
        result_ref[rows, :] = value.astype(BF16)


def norm_back(partial_sum, out, hidden, grad_rows, gain, n_head):
    rows_here, model = hidden.shape
    span, outer = model // n_head, n_head // 2
    return pl.pallas_call(
        norm_kernel,
        out_shape=[
            shape((rows_here, span), BF16),
            shape((rows_here, span), F32),
            shape((rows_here, model), BF16),
            shape((1, span), F32),
        ],
        in_specs=[VMEM] * 5,
        out_specs=[VMEM] * 4,
        scratch_shapes=[
            pltpu.VMEM((rows_here, model), BF16),
            pltpu.VMEM((outer, rows_here, span), BF16),
            pltpu.VMEM((outer, outer, rows_here, span), BF16),
            pltpu.VMEM((outer, rows_here, span), BF16),
            pltpu.VMEM((outer, rows_here, span), BF16),
            DMA((2, outer)),
            DMA((2, outer)),
            DMA((2, outer)),
            DMA((2, outer)),
            DMA((outer,)),
            DMA((outer,)),
        ],
        compiler_params=pltpu.CompilerParams(
            collective_id=4, has_side_effects=True, vmem_limit_bytes=VMEM_BYTES
        ),
        name="second_norm_back",
    )(partial_sum, out, hidden, grad_rows, gain)


def gate_back_kernel(
    branch_ref,
    w_out_ref,
    out_ref,
    proj_ref,
    gain_ref,
    reach_ref,
    map_ref,
    grad_out_ref,
    grad_gate_ref,
    grad_gain_ref,
    residual_ref,
    total_ref,
):
    heads, groups = reach_ref.shape[:2]
    block = proj_ref.shape[1] // heads
    grad_gain_ref[...] = jnp.zeros_like(grad_gain_ref)
    for head in range(heads):
        total_ref[head] = jnp.zeros((WIDTH, WIDTH), F32)

    @pl.loop(0, groups)
    def _(turn):
        group = groups - 1 - turn
        rows = pl.ds(pl.multiple_of(group * GROUP, GROUP), GROUP)
        shifted = pl.ds(pl.multiple_of(group * GROUP + RIM, RIM), GROUP)
        grad_gated = dot(branch_ref[rows, :], w_out_ref[...])
        for head in range(heads):
            span = slice(head * WIDTH, (head + 1) * WIDTH)
            gain = gain_ref[:, span]
            out = out_ref[rows, span]
            scale = lax.rsqrt(row_sum(out * out) / WIDTH + EPSILON)
            gate = proj_ref[shifted, (head + 1) * block - WIDTH : (head + 1) * block]
            sigma = jax.nn.sigmoid(gate)
            grad = grad_gated[:, span]
            scaled = out * scale
            grad_normed = grad * gate * sigma
            grad_gate_ref[rows, span] = (
                grad * scaled * gain * sigma * (1.0 + gate * (1.0 - sigma))
            ).astype(BF16)
            grad_gain_ref[:, span] += jnp.sum(grad_normed * scaled, axis=0, keepdims=True)
            weighted = grad_normed * gain
            grad_out = scale * (weighted - scaled * (row_sum(weighted * scaled) / WIDTH))
            grad_out_ref[rows, span] = grad_out
            residual = dot_mid(reach_ref[head, group], grad_out, (0, 0))
            residual_ref[head, group] = residual
            total_ref[head] = residual + dot_mid(map_ref[head, group], total_ref[head], (0, 0))


def gate_back(branch, w_out, out, proj, gain, reach, maps):
    heads, groups = reach.shape[:2]
    rows_here = branch.shape[0]
    return pl.pallas_call(
        gate_back_kernel,
        out_shape=[
            shape((rows_here, heads * WIDTH), F32),
            shape((rows_here, heads * WIDTH), BF16),
            shape((1, heads * WIDTH), F32),
            shape((heads, groups, WIDTH, WIDTH), F32),
            shape((heads, WIDTH, WIDTH), F32),
        ],
        in_specs=[VMEM] * 7,
        out_specs=[VMEM] * 5,
        compiler_params=pltpu.CompilerParams(vmem_limit_bytes=VMEM_BYTES),
        name="mixer_gate_back",
    )(branch, w_out, out, proj, gain, reach, maps)


def mixer_back_kernel(
    lengths_ref,
    rate_ref,
    adjoint_ref,
    proj_ref,
    small_ref,
    taps_ref,
    query_ref,
    key_ref,
    value_ref,
    inverse_ref,
    solved_ref,
    lower_ref,
    scores_ref,
    starts_ref,
    map_ref,
    grad_out_ref,
    residual_ref,
    grad_proj_ref,
    grad_small_ref,
    grad_taps_ref,
    grad_rate_ref,
    running,
):
    heads, groups = key_ref.shape[:2]
    block = proj_ref.shape[1] // heads
    channels = (1 + 2 * HOUSE) * WIDTH
    rows_here = groups * GROUP
    first = lax.axis_index("seq") * rows_here
    bounds = bounds_of(lengths_ref)
    grad_proj_ref[...] = jnp.zeros_like(grad_proj_ref)
    grad_taps_ref[...] = jnp.zeros_like(grad_taps_ref)
    grad_rate_ref[...] = jnp.zeros_like(grad_rate_ref)
    running[...] = adjoint_ref[...]

    @pl.loop(0, groups)
    def _(turn):
        group = groups - 1 - turn
        keeps = conv_keeps(group, first, bounds)
        masks = group_masks(group, first, bounds)
        rows = pl.ds(pl.multiple_of(group * GROUP, GROUP), GROUP)
        small_parts = []
        for head in range(heads):
            span = slice(head * WIDTH, (head + 1) * WIDTH)
            betas, decay_logit, soft, cumulative = gate_terms(
                small_ref, rate_ref[head], group, head
            )
            beta = jnp.concatenate([betas[:, 0:1], betas[:, 1:2]], axis=0)
            decay, growth, to_end = decay_terms(cumulative, masks)
            query, keys, values = query_ref[head, group], key_ref[head, group], value_ref[head, group]
            lower, scores = lower_ref[head, group], scores_ref[head, group]
            solved, start = solved_ref[head, group], starts_ref[head, group]
            grad_out = grad_out_ref[rows, span]
            after = running[head]
            running[head] = residual_ref[head, group] + dot_mid(map_ref[head, group], after, (0, 0))
            updates = solved[:, :WIDTH] - dot_mid(solved[:, WIDTH:], start)
            carried = to_end * keys
            grad_reach = dot_mid(grad_out, start, (1, 1))
            grad_scores = dot_mid(grad_out, updates, (1, 1))
            grad_updates = dot_mid(scores, grad_out, (0, 0)) + dot_mid(carried, after)
            grad_carried = dot_mid(updates, after, (1, 1))
            grad_total = jnp.sum(row_sum(start * after), axis=0, keepdims=True)
            grad_pull = -dot_mid(grad_updates, start, (1, 1))
            right = dot_mid(
                inverse_ref[head, group],
                jnp.concatenate([grad_updates, grad_pull], axis=1),
                (0, 0),
            )
            grad_lower = jnp.where(masks[1], -dot_mid(right, solved, (1, 1)), 0.0)
            right_value, right_key = right[:, :WIDTH], right[:, WIDTH:]
            grad_values = beta * right_value
            by_key = row_sum(right_key * keys)
            weighted = grad_lower * lower
            grad_beta = row_sum(right_value * values) + by_key * growth
            inner_decay = decay * dot_mid(keys, keys, (1, 1))
            grad_beta = grad_beta + row_sum(grad_lower * inner_decay)
            grad_growth = by_key * beta
            grad_inner = grad_lower * decay * beta
            pairs = grad_scores * decay[GROUP:]
            grad_query = growth[GROUP:] * grad_reach + dot_mid(pairs, keys)
            grad_keys = (
                (beta * growth) * right_key
                + to_end * grad_carried
                + dot_mid(pairs, query, (0, 0))
                + dot_mid(grad_inner, keys)
                + dot_mid(grad_inner, keys, (0, 0))
            )
            by_end = row_sum(grad_carried * keys) * to_end
            by_reach = row_sum(grad_reach * query)
            score_part = grad_scores * scores
            spread = weighted + jnp.concatenate([jnp.zeros_like(score_part), score_part], axis=0)
            is_last = rows_of(MICRO) == MICRO - 1
            grad_growth = grad_growth + jnp.concatenate([jnp.zeros_like(by_reach), by_reach], axis=0)
            grad_growth = grad_growth + jnp.where(is_last, grad_total, 0.0)
            column = row_sum(spread) - by_end + grad_growth * growth
            column = column + jnp.where(is_last, jnp.sum(by_end, axis=0, keepdims=True), 0.0)
            column = column - to_column(jnp.sum(spread, axis=0, keepdims=True))
            per_token = column[:GROUP] + column[GROUP:]
            later = lanes_of(GROUP) >= rows_of(GROUP)
            grad_log_decay = row_sum(jnp.where(later, to_lane(per_token), 0.0))
            rate = rate_ref[head]
            grad_rate_ref[0:1, head : head + 1] += jnp.sum(
                -grad_log_decay * soft, axis=0, keepdims=True
            )
            grad_logit = -rate * grad_log_decay * jax.nn.sigmoid(decay_logit)
            grad_beta = grad_beta * beta * (1.0 - 0.5 * beta)
            small_parts += [grad_beta[:GROUP], grad_beta[GROUP:], grad_logit]
            grads = [
                grad_query,
                grad_keys[:GROUP],
                grad_keys[GROUP:],
                grad_values[:GROUP],
                grad_values[GROUP:],
            ]
            units = [query, keys[:GROUP], keys[GROUP:]]
            for part, grad in enumerate(grads):
                column_at = head * block + part * WIDTH
                taps_at = head * channels + part * WIDTH
                parts = conv_window(proj_ref, group, column_at)
                total = conv_total(parts, keeps, taps_ref, taps_at)
                sigma = jax.nn.sigmoid(total)
                if part < 1 + HOUSE:
                    mixed = total * sigma
                    scale = lax.rsqrt(row_sum(mixed * mixed) + EPSILON)
                    unit = units[part]
                    grad = scale * (grad - unit * row_sum(grad * unit))
                grad = grad * sigma * (1.0 + total * (1.0 - sigma))
                taps_span = slice(taps_at, taps_at + WIDTH)
                window = jnp.zeros((GROUP + 8, WIDTH), F32)
                for step in range(4):
                    kept = grad if step == 0 else grad * keeps[step]
                    grad_taps_ref[step : step + 1, taps_span] += jnp.sum(
                        kept * parts[step], axis=0, keepdims=True
                    )
                    moved = kept * taps_ref[step : step + 1, taps_span]
                    pieces = [jnp.zeros((8 - step, WIDTH), F32), moved]
                    if step:
                        pieces.append(jnp.zeros((step, WIDTH), F32))
                    window = window + jnp.concatenate(pieces, axis=0)
                place = pl.ds(pl.multiple_of(group * GROUP + RIM - 8, 8), GROUP + 8)
                grad_proj_ref[place, taps_span] += window
        padding = jnp.zeros((GROUP, WIDTH - len(small_parts)), F32)
        grad_small_ref[rows, :] = jnp.concatenate(small_parts + [padding], axis=1).astype(BF16)


def mixer_back(
    lengths,
    rate,
    adjoint,
    proj,
    small,
    taps,
    query,
    keys,
    values,
    inverse,
    solved,
    lower,
    scores,
    starts,
    maps,
    grad_out,
    residual,
):
    heads, groups = keys.shape[:2]
    rows_here = groups * GROUP
    channels = taps.shape[1]
    return pl.pallas_call(
        mixer_back_kernel,
        out_shape=[
            shape((rows_here + RIM, channels), F32),
            shape((rows_here, WIDTH), BF16),
            shape((8, channels), F32),
            shape((8, WIDTH), F32),
        ],
        in_specs=[SMEM, SMEM] + [VMEM] * 15,
        out_specs=[VMEM] * 4,
        scratch_shapes=[pltpu.VMEM((heads, WIDTH, WIDTH), F32)],
        compiler_params=pltpu.CompilerParams(vmem_limit_bytes=VMEM_BYTES),
        name="mixer_back",
    )(
        lengths,
        rate,
        adjoint,
        proj,
        small,
        taps,
        query,
        keys,
        values,
        inverse,
        solved,
        lower,
        scores,
        starts,
        maps,
        grad_out,
        residual,
    )


def spread_kernel(count, *refs):
    refs = list(refs)
    take = lambda number: [refs.pop(0) for _ in range(number)]
    partials, outs, sides, ups, downs = (take(count) for _ in range(5))
    side_sends, side_receives, way_sends, way_receives = take(4)
    me_seq, me_head, outer, place, inner = seq_links()
    greet(seq_neighbours())

    def to_side(at, far):
        return remote(
            partials[at].at[2 * far + 1 - inner],
            sides[at].at[far],
            side_sends.at[at, far],
            side_receives.at[at, far],
            (other_of(me_seq), me_head),
        )

    def up(at, far):
        return remote(
            sides[at].at[far],
            ups[at].at[far],
            way_sends.at[0, at, far],
            way_receives.at[0, at, far],
            (me_seq + 2, me_head),
        )

    def down(at, far):
        return remote(
            sides[at].at[far],
            downs[at].at[far],
            way_sends.at[1, at, far],
            way_receives.at[1, at, far],
            (me_seq - 2, me_head),
        )

    def add(at, far, terms, target):
        depth = partials[at].shape[1]
        tile = min(depth, 64)

        @pl.loop(0, depth // tile)
        def _(turn):
            rows = pl.ds(pl.multiple_of(turn * tile, tile), tile)
            total = terms[0](rows).astype(F32)
            for term in terms[1:]:
                total = total + term(rows).astype(F32)
            target(rows, total)

    order = sorted(range(outer), key=lambda far: -abs(2 * far + 1 - outer))
    for far in order:
        for at in range(count):
            to_side(at, far).start()
    for far in order:
        for at in range(count):
            to_side(at, far).wait_recv()

            def keep(rows, total, at=at, far=far):
                sides[at][far, rows, :] = total.astype(sides[at].dtype)

            mine = lambda rows, at=at, far=far: partials[at][2 * far + inner, rows, :]
            side = lambda rows, at=at, far=far: sides[at][far, rows, :]
            add(at, far, [mine, side], keep)

            @pl.when(far > place)
            def _():
                @pl.when(place > 0)
                def _():
                    up(at, far).wait_recv()
                    below = lambda rows, at=at, far=far: ups[at][far, rows, :]
                    add(at, far, [side, below], keep)

                up(at, far).start()

            @pl.when(far < place)
            def _():
                @pl.when(place < outer - 1)
                def _():
                    down(at, far).wait_recv()
                    above = lambda rows, at=at, far=far: downs[at][far, rows, :]
                    add(at, far, [side, above], keep)

                down(at, far).start()

    for at in range(count):

        def store(rows, total, at=at):
            outs[at][rows, :] = total

        side = lambda rows, at=at: sides[at][place, rows, :]
        below = lambda rows, at=at: ups[at][place, rows, :]
        above = lambda rows, at=at: downs[at][place, rows, :]

        @pl.when(place > 0)
        def _():
            up(at, place).wait_recv()

        @pl.when(place < outer - 1)
        def _():
            down(at, place).wait_recv()

        @pl.when(place == 0)
        def _():
            add(at, place, [side, above], store)

        @pl.when(place == outer - 1)
        def _():
            add(at, place, [side, below], store)

        @pl.when((place > 0) & (place < outer - 1))
        def _():
            add(at, place, [side, below, above], store)

    for at in range(count):
        for far in range(outer):
            to_side(at, far).wait_send()

            @pl.when(far > place)
            def _():
                up(at, far).wait_send()

            @pl.when(far < place)
            def _():
                down(at, far).wait_send()


def spread_sums(partials):
    count = len(partials)
    n_seq = partials[0].shape[0]
    outer = n_seq // 2
    buffers = [pltpu.VMEM((outer,) + a.shape[1:], a.dtype) for a in partials]
    return pl.pallas_call(
        partial(spread_kernel, count),
        out_shape=[shape(a.shape[1:], F32) for a in partials],
        in_specs=[VMEM] * count,
        out_specs=[VMEM] * count,
        scratch_shapes=buffers * 3
        + [
            DMA((count, outer)),
            DMA((count, outer)),
            DMA((2, count, outer)),
            DMA((2, count, outer)),
        ],
        compiler_params=pltpu.CompilerParams(
            collective_id=5, has_side_effects=True, vmem_limit_bytes=VMEM_BYTES
        ),
        name="sums_over_seq",
    )(*partials)


def entry_back_kernel(
    partial_ref,
    inner_ref,
    columns_ref,
    rows_ref,
    gain_ref,
    grad_hidden_ref,
    grad_ref,
    grad_gain_ref,
    cores,
    chips,
    inner_core,
    inner_chips,
    sends,
    receives,
    chip_sends,
    chip_receives,
):
    rows_here, model = partial_ref.shape
    me_seq, me_head = lax.axis_index("seq"), lax.axis_index("head")
    outer = lax.axis_size("head") // 2
    chip = me_head // 2
    greet(head_neighbours())
    back = HeadSum(partial_ref, cores, chips, sends, receives)
    back.start()

    def inner_to_core():
        return remote(
            inner_ref,
            inner_core,
            sends.at[outer],
            receives.at[outer],
            (me_seq, other_of(me_head)),
        )

    def to_chip(step):
        target = lax.rem(me_head + 2 * step, 2 * outer)
        return remote(
            cores.at[target // 2],
            chips.at[step],
            chip_sends.at[0, step],
            chip_receives.at[0, step],
            (me_seq, target),
        )

    def inner_to_chip(step):
        return remote(
            inner_core,
            inner_chips.at[step],
            chip_sends.at[1, step],
            chip_receives.at[1, step],
            (me_seq, lax.rem(me_head + 2 * step, 2 * outer)),
        )

    inner_to_core().start()
    for at in range(outer):
        back.add_core(at)
    inner_to_core().wait()
    inner_core[...] = inner_core[...] + inner_ref[...]
    for step in range(1, outer):
        inner_to_chip(step).start()
        to_chip(step).start()
    for step in range(1, outer):
        inner_to_chip(step).wait()
        to_chip(step).wait()
    inner_total = inner_core[...]
    for step in range(1, outer):
        inner_total = inner_total + inner_chips[step]
    inner_core[...] = inner_total
    span = model // (2 * outer)
    own = pl.ds(pl.multiple_of(me_head * span, span), span)
    grad_gain_ref[...] = jnp.zeros_like(grad_gain_ref)
    tile = 128

    @pl.loop(0, rows_here // tile)
    def _(turn):
        rows = pl.ds(pl.multiple_of(turn * tile, tile), tile)
        whole = rows_ref[rows, :].astype(F32)
        scale = lax.rsqrt(row_sum(whole * whole) / model + EPSILON)
        inner = to_column(inner_core[pl.ds(turn, 1), :])
        total = cores[chip, rows, :].astype(F32)
        for step in range(1, outer):
            total = total + chips[step, rows, :].astype(F32)
        values = columns_ref[rows, :].astype(F32)
        grad = scale * total * gain_ref[:, own] - values * (scale * scale * scale * inner / model)
        grad_ref[rows, :] = grad + grad_hidden_ref[rows, :]
        grad_gain_ref[...] += jnp.sum(total * values * scale, axis=0, keepdims=True)


def entry_back(partial_sum, inner, columns, rows, gain, grad_hidden, n_head):
    rows_here, model = rows.shape
    span, outer = model // n_head, n_head // 2
    return pl.pallas_call(
        entry_back_kernel,
        out_shape=[shape((rows_here, span), F32), shape((1, span), F32)],
        in_specs=[VMEM] * 6,
        out_specs=[VMEM] * 2,
        scratch_shapes=[
            pltpu.VMEM((outer, rows_here, span), BF16),
            pltpu.VMEM((outer, rows_here, span), BF16),
            pltpu.VMEM(inner.shape, F32),
            pltpu.VMEM((outer,) + inner.shape, F32),
            DMA((outer + 1,)),
            DMA((outer + 1,)),
            DMA((2, outer)),
            DMA((2, outer)),
        ],
        compiler_params=pltpu.CompilerParams(
            collective_id=6, has_side_effects=True, vmem_limit_bytes=VMEM_BYTES
        ),
        name="first_norm_back",
    )(partial_sum, inner, columns, rows, gain, grad_hidden)


def tiled(flat, rows):
    return jnp.pad(flat, (0, rows * WIDTH - flat.shape[0])).reshape(rows, WIDTH)


def on_device(
    n_seq,
    n_head,
    inputs,
    lengths,
    norm1_gain,
    w_in,
    w_small,
    conv_weight,
    decay_rate,
    out_gain,
    w_out,
    norm2_gain,
    w_gate,
    w_up,
    w_down,
    cotangent,
):
    rows_here, span = inputs.shape
    model = span * n_head
    heads = decay_rate.shape[0]
    small_count = w_small.shape[1]
    me_head = lax.axis_index("head")

    pieces = [norm1_gain, norm2_gain, out_gain, conv_weight.reshape(-1), w_small.reshape(-1)]
    sizes = [piece.shape[0] for piece in pieces]
    tile_rows = -(-sum(sizes) // (16 * WIDTH)) * 16
    tile = tiled(jnp.concatenate(pieces), tile_rows)
    shards = [tile, w_out.T, w_in, w_gate, w_up, w_down.T]
    rows, grad_rows, rim, gathered, wide = entry(inputs, cotangent, shards, 2, n_seq, n_head)
    flat = wide[0].reshape(n_head, n_seq, -1)
    cuts = [0]
    for size in sizes:
        cuts.append(cuts[-1] + size)
    piece_of = lambda at: flat[:, :, cuts[at] : cuts[at + 1]]
    gain_one = piece_of(0).reshape(1, model).astype(F32)
    gain_two = piece_of(1).reshape(1, model).astype(F32)
    mine = lax.dynamic_index_in_dim(flat, me_head, 0, keepdims=False)
    own_of = lambda at: mine[:, cuts[at] : cuts[at + 1]]
    gain_heads = own_of(2).reshape(1, heads * WIDTH).astype(F32)
    taps = jnp.swapaxes(own_of(3).reshape(n_seq, 4, -1), 0, 1).reshape(4, -1).astype(F32)
    proj_small = jnp.pad(own_of(4).reshape(model, small_count), ((0, 0), (0, WIDTH - small_count)))
    w_out_all = wide[1].reshape(n_head, model, -1)
    w_out_own = gathered[1].reshape(model, -1)
    proj_in = gathered[2].reshape(model, -1)
    gate_in = gathered[3].reshape(model, -1)
    up_in = gathered[4].reshape(model, -1)
    down = gathered[5].reshape(model, -1)

    (
        normed_one,
        proj,
        small,
        query,
        keys,
        values,
        inverse,
        solved,
        lower,
        scores,
        reach,
        local,
        maps,
        adds,
        before,
        total,
    ) = mixer(lengths, decay_rate, rows, rim, gain_one, proj_in, proj_small, taps)
    state, pair, aside = carry_state(total)
    gated, starts, out = gated_output(state, before, local, reach, proj, gain_heads, rows_here)
    gated_rows = gather_rows(gated, n_head)
    hidden, normed_two, inner, out_part, grad_gate, grad_up, back_part = feed_forward(
        rows, gated_rows, w_out_all, gain_two, gate_in, up_in, down, grad_rows
    )
    result, grad_hidden, branch, grad_gain_two = norm_back(
        back_part, out_part, hidden, grad_rows, gain_two, n_head
    )
    grad_mixed, grad_gate_part, grad_gain_heads, residual, residual_total = gate_back(
        branch, w_out_own, out, proj, gain_heads, reach, maps
    )
    own_map = total[:, :, :WIDTH].astype(BF16).astype(F32)
    adjoint = carry_adjoint(
        residual_total, jnp.concatenate([pair[:, :, :WIDTH], own_map], axis=2), aside
    )
    grad_conv, grad_small, grad_taps, grad_rate = mixer_back(
        lengths,
        decay_rate,
        adjoint,
        proj,
        small,
        taps,
        query,
        keys,
        values,
        inverse,
        solved,
        lower,
        scores,
        starts,
        maps,
        grad_mixed,
        residual,
    )
    back_links = [(source, source - 1) for source in range(1, n_seq)]
    returned = lax.ppermute(grad_conv[RIM - 3 : RIM], "seq", back_links)
    grad_conv = grad_conv[RIM:].at[rows_here - 3 :].add(returned)
    grad_projected = jnp.concatenate(
        [
            grad_conv.reshape(rows_here, heads, -1).astype(BF16),
            grad_gate_part.reshape(rows_here, heads, -1),
        ],
        axis=2,
    ).reshape(rows_here, -1)
    grad_proj_in = jnp.dot(normed_one[RIM:].T, grad_projected, preferred_element_type=F32)
    grad_proj_small = jnp.dot(normed_one[RIM:].T, grad_small, preferred_element_type=F32)
    back_one = jnp.dot(grad_projected, proj_in.T, preferred_element_type=F32) + jnp.dot(
        grad_small, proj_small.T, preferred_element_type=F32
    )
    inner_one = jnp.sum(back_one * gain_one * rows.astype(F32), axis=1).reshape(-1, WIDTH)
    grad_inputs, grad_gain_one = entry_back(
        back_one.astype(BF16), inner_one, inputs, rows, gain_one, grad_hidden, n_head
    )
    grad_down = jnp.dot(grad_rows.T, inner, preferred_element_type=F32)
    grad_gate_in = jnp.dot(normed_two.T, grad_gate, preferred_element_type=F32)
    grad_up_in = jnp.dot(normed_two.T, grad_up, preferred_element_type=F32)
    grad_out = jnp.dot(branch.T, gated, preferred_element_type=F32)
    stacked = lambda values: values.astype(BF16).reshape(n_seq, -1, values.shape[1])
    taps_out = jnp.swapaxes(grad_taps[:4].reshape(4, n_seq, -1), 0, 1).reshape(n_seq, -1)
    rates = jnp.broadcast_to(grad_rate[0:1, :heads], (n_seq, heads))
    tail = jnp.concatenate(
        [
            grad_gain_one.reshape(n_seq, -1),
            grad_gain_two.reshape(n_seq, -1),
            grad_gain_heads.reshape(n_seq, -1),
            taps_out,
            grad_proj_small[:, :small_count].reshape(n_seq, -1),
            rates,
        ],
        axis=1,
    )
    tail_rows = -(-tail.shape[1] // (8 * WIDTH)) * 8
    tail = jnp.pad(tail, ((0, 0), (0, tail_rows * WIDTH - tail.shape[1])))
    sums = spread_sums(
        [
            stacked(grad_gate_in),
            stacked(grad_up_in),
            stacked(grad_down),
            stacked(grad_out),
            stacked(grad_proj_in),
            tail.reshape(n_seq, tail_rows, WIDTH),
        ]
    )
    flat_out = sums[5].reshape(-1)
    cut = lambda at: flat_out[cuts[at] : cuts[at + 1]]
    return (
        result,
        grad_inputs,
        cut(0),
        sums[4],
        cut(4).reshape(-1, small_count),
        cut(3).reshape(4, -1),
        flat_out[cuts[5] : cuts[5] + heads],
        cut(2),
        sums[3].T,
        cut(1),
        sums[0],
        sums[1],
        sums[2].T,
    )


def solution(mesh):
    return jax.shard_map(
        partial(on_device, mesh.shape["seq"], mesh.shape["head"]),
        mesh=mesh,
        in_specs=(
            P("seq", "head"),
            P(),
            P(("head", "seq")),
            P("seq", "head"),
            P("seq", "head"),
            P(None, ("head", "seq")),
            P("head"),
            P(("head", "seq")),
            P("head", "seq"),
            P(("head", "seq")),
            P("seq", "head"),
            P("seq", "head"),
            P("head", "seq"),
            P("seq", "head"),
        ),
        out_specs=(
            P("seq", "head"),
            P("seq", "head"),
            P(("head", "seq")),
            P("seq", "head"),
            P("seq", "head"),
            P(None, ("head", "seq")),
            P("head"),
            P(("head", "seq")),
            P("head", "seq"),
            P(("head", "seq")),
            P("seq", "head"),
            P("seq", "head"),
            P("head", "seq"),
        ),
        check_vma=False,
    )
```

```python
from functools import partial
from types import SimpleNamespace

import jax
import jax.numpy as jnp
from jax import lax
from jax.experimental import pallas as pl
from jax.experimental.pallas import tpu as pltpu
from jax.sharding import PartitionSpec as P

HOUSE = 2
GROUP = 64
MICRO = GROUP * HOUSE
WIDTH = 128
RIM = 16
EPSILON = 1e-06
MESH = pl.DeviceIdType.MESH
VMEM_BYTES = 60 * 2**20
F32 = jnp.float32
BF16 = jnp.bfloat16

VMEM = pl.BlockSpec(memory_space=pltpu.VMEM)
SMEM = pl.BlockSpec(memory_space=pltpu.SMEM)
ANY = pl.BlockSpec(memory_space=pl.ANY)
DMA = pltpu.SemaphoreType.DMA


def shape(dims, kind):
    return jax.ShapeDtypeStruct(tuple(dims), kind)


def dot(left, right, over=(1, 0)):
    return lax.dot_general(
        left, right, (((over[0],), (over[1],)), ((), ())), preferred_element_type=F32
    )


def dot_low(left, right, over=(1, 0)):
    return dot(left.astype(BF16), right.astype(BF16), over)


def halves(values):
    high = values.astype(BF16)
    return high, (values - high.astype(F32)).astype(BF16)


def dot_mid(left, right, over=(1, 0)):
    left_high, left_low = halves(left)
    right_high, right_low = halves(right)
    return (
        dot(left_high, right_low, over)
        + dot(left_low, right_high, over)
        + dot(left_high, right_high, over)
    )


def rows_of(count):
    return lax.broadcasted_iota(jnp.int32, (count, 1), 0)


def lanes_of(count):
    return lax.broadcasted_iota(jnp.int32, (1, count), 1)


def to_lane(column):
    count = column.shape[0]
    return jnp.sum(jnp.where(rows_of(count) == lanes_of(count), column, 0.0), axis=0, keepdims=True)


def to_column(lane):
    count = lane.shape[1]
    return jnp.sum(jnp.where(rows_of(count) == lanes_of(count), lane, 0.0), axis=1, keepdims=True)


def row_sum(values):
    return jnp.sum(values, axis=1, keepdims=True)


def bounds_of(lengths_ref):
    bounds = []
    total = 0
    for at in range(lengths_ref.shape[0]):
        total = total + lengths_ref[at]
        bounds.append(total)
    return bounds


def owner_of(positions, bounds):
    total = jnp.zeros_like(positions)
    for bound in bounds:
        total = total + (bound <= positions).astype(jnp.int32)
    return total


def micro_order(index):
    return 2 * (index & (GROUP - 1)) + lax.shift_right_logical(index, 6)


def level_masks():
    above, left = micro_order(rows_of(MICRO)), micro_order(lanes_of(MICRO))
    found = []
    for level in range(7):
        step = 1 << level
        found.append(
            (lax.shift_right_logical(above, level + 1) == lax.shift_right_logical(left, level + 1))
            & ((above & step) != 0)
            & ((left & step) == 0)
        )
    return found


def unit_inverse(lowers, masks_ref):
    eye = (rows_of(MICRO) == lanes_of(MICRO)).astype(F32)
    split = [halves(lower) for lower in lowers]
    first = masks_ref[0].astype(F32)
    found = [eye - first * lower for lower in lowers]
    for level in range(1, 7):
        mask = masks_ref[level]
        inner = []
        parts = [halves(value) for value in found]
        for (high, low), (to_high, to_low) in zip(split, parts):
            off_high, off_low = high * mask, low * mask
            inner.append(dot(off_high, to_low) + dot(off_low, to_high) + dot(off_high, to_high))
        for at, (value, (to_high, to_low)) in enumerate(zip(inner, parts)):
            high, low = halves(value)
            found[at] = found[at] - (dot(to_high, low) + dot(to_low, high) + dot(to_high, high))
    return found


def conv_window(proj_ref, group, column):
    start = pl.multiple_of(group * GROUP + RIM - 8, 8)
    window = proj_ref[pl.ds(start, GROUP + 8), pl.ds(column, WIDTH)]
    return [window[8 - step : GROUP + 8 - step] for step in range(4)]


def conv_total(parts, keeps, taps):
    total = parts[0] * taps[0:1]
    for step in range(1, 4):
        total = total + parts[step] * keeps[step] * taps[step : step + 1]
    return total


OWNER_ROW, KEEP_ROW, TABLE_ROWS = 8, 9, 16


def group_columns(table_t_ref, group, heads):
    columns = table_t_ref[group]
    keeps = [None] + [columns[:GROUP, KEEP_ROW + at : KEEP_ROW + at + 1] for at in range(3)]
    return columns, keeps


def decay_of(columns, table, head, reach):
    at = 4 * head + 1
    spread = jnp.minimum(columns[:, at : at + 1] - table[at : at + 1, :], 0.0)
    return jnp.where(reach, jnp.exp(spread), 0.0)


def reach_of(columns, table):
    same = columns[:, OWNER_ROW : OWNER_ROW + 1] == table[OWNER_ROW : OWNER_ROW + 1, :]
    return same & (micro_order(lanes_of(MICRO)) <= micro_order(rows_of(MICRO)))


def soft_plus(logits):
    return jnp.maximum(logits, 0.0) + jnp.log(1.0 + jnp.exp(-jnp.abs(logits)))


def fill_tables(logits, rates, heads, groups, first, bounds, table_ref, table_t_ref):
    betas = 2.0 * jax.nn.sigmoid(logits)
    so_far = -soft_plus(logits)
    within = lanes_of(logits.shape[1]) & (GROUP - 1)
    step = 1
    while step < GROUP:
        so_far = so_far + jnp.where(within >= step, pltpu.roll(so_far, step, 1), 0.0)
        step *= 2
    token = lanes_of(MICRO) & (GROUP - 1)
    for group in range(groups):
        span = slice(group * GROUP, (group + 1) * GROUP)
        start = first + group * GROUP
        owners = owner_of(start + token, bounds)
        prior = owner_of(jnp.full((1, 1), start - 1, jnp.int32), bounds)
        last = owner_of(jnp.full((1, 1), start + GROUP - 1, jnp.int32), bounds)
        carries = (owners == prior).astype(F32)
        ends = (owners == last).astype(F32)
        table = []
        for head in range(2):
            if head >= heads:
                table.append(jnp.zeros((4, MICRO), F32))
                continue
            at = head * (HOUSE + 1)
            beta = jnp.concatenate([betas[at : at + 1, span], betas[at + 1 : at + 2, span]], axis=1)
            decay = rates[head] * so_far[at + HOUSE : at + HOUSE + 1, span]
            decay = jnp.concatenate([decay, decay], axis=1)
            final = decay[:, MICRO - 1 : MICRO]
            growth = jnp.exp(decay) * carries
            to_end = ends * jnp.exp(jnp.minimum(final - decay, 0.0))
            table += [beta, decay, growth, to_end]
        table.append(owners.astype(F32))
        for step in range(1, 4):
            table.append((owner_of(start + token - step, bounds) == owners).astype(F32))
        table.append(jnp.zeros((TABLE_ROWS - KEEP_ROW - 3, MICRO), F32))
        table = jnp.concatenate(table, axis=0)
        table_ref[group] = table
        table_t_ref[group] = jnp.transpose(table)


def seq_links():
    me_seq, me_head = lax.axis_index("seq"), lax.axis_index("head")
    outer = lax.axis_size("seq") // 2
    place, inner = me_seq // 2, lax.rem(me_seq, 2)
    return me_seq, me_head, outer, place, inner


def other_of(index):
    return index + 1 - 2 * lax.rem(index, 2)


def greet(devices):
    barrier = pltpu.get_barrier_semaphore()
    count = 0
    for condition, device in devices:
        if condition is None:
            pl.semaphore_signal(barrier, inc=1, device_id=device, device_id_type=MESH)
            count = count + 1
        else:

            @pl.when(condition)
            def _():
                pl.semaphore_signal(barrier, inc=1, device_id=device, device_id_type=MESH)

            count = count + jnp.where(condition, 1, 0)
    pl.semaphore_wait(barrier, count)


def seq_neighbours():
    me_seq, me_head, outer, place, inner = seq_links()
    return [
        (None, (other_of(me_seq), me_head)),
        (place < outer - 1, (me_seq + 2, me_head)),
        (place > 0, (me_seq - 2, me_head)),
    ]


def head_neighbours():
    me_seq, me_head = lax.axis_index("seq"), lax.axis_index("head")
    outer = lax.axis_size("head") // 2
    found = [(None, (me_seq, other_of(me_head)))]
    for step in range(1, outer):
        found.append((None, (me_seq, lax.rem(me_head + 2 * step, 2 * outer))))
    return found


def remote(source, target, send, receive, device):
    return pltpu.make_async_remote_copy(
        src_ref=source,
        dst_ref=target,
        send_sem=send,
        recv_sem=receive,
        device_id=device,
        device_id_type=MESH,
    )


class SeqGather:
    def __init__(self, source, place_of, sends, receives):
        self.source, self.block = source, place_of
        self.sends, self.receives = sends, receives
        self.next = 1

    def send(self, origin, way, device, source=None):
        source = self.block(origin) if source is None else source
        remote(
            source, self.block(origin), self.sends.at[origin, way], self.receives.at[origin], device
        ).start()

    def wait_send(self, origin, way):
        me_seq, me_head, outer, place, inner = seq_links()
        remote(
            self.block(origin),
            self.block(origin),
            self.sends.at[origin, way],
            self.receives.at[origin],
            (me_seq, me_head),
        ).wait_send()

    def wait_arrival(self, origin):
        me_seq, me_head, outer, place, inner = seq_links()
        remote(
            self.block(origin),
            self.block(origin),
            self.sends.at[origin, 0],
            self.receives.at[origin],
            (me_seq, me_head),
        ).wait_recv()

    def start(self, local):
        me_seq, me_head, outer, place, inner = seq_links()
        self.local = pltpu.make_async_copy(self.source, self.block(me_seq), local)
        self.local.start()

        @pl.when(place < outer - 1)
        def _():
            self.send(me_seq, 0, (me_seq + 2, me_head), self.source)

        @pl.when(place > 0)
        def _():
            self.send(me_seq, 1, (me_seq - 2, me_head), self.source)

        self.send(me_seq, 2, (other_of(me_seq), me_head), self.source)

    def relay(self, step):
        me_seq, me_head, outer, place, inner = seq_links()
        below, above = me_seq - 2 * step, me_seq + 2 * step
        aside = (other_of(me_seq), me_head)

        @pl.when(place >= step)
        def _():
            self.wait_arrival(below)

            @pl.when(place < outer - 1)
            def _():
                self.send(below, 0, (me_seq + 2, me_head))

            self.send(below, 2, aside)

        @pl.when(place < outer - step)
        def _():
            self.wait_arrival(above)

            @pl.when(place > 0)
            def _():
                self.send(above, 1, (me_seq - 2, me_head))

            self.send(above, 2, aside)

    def advance(self):
        if self.next < lax.axis_size("seq") // 2:
            self.relay(self.next)
            self.next += 1

    def drain(self):
        while self.next < lax.axis_size("seq") // 2:
            self.advance()

    def finish(self, local=True, arrivals=True):
        me_seq, me_head, outer, place, inner = seq_links()
        if local:
            self.local.wait()
        for at in range(outer):
            if arrivals:
                self.wait_arrival(2 * at + 1 - inner)
        for at in range(outer):
            origin = 2 * at + inner
            self.wait_send(origin, 2)

            @pl.when((at <= place) & (place < outer - 1))
            def _():
                self.wait_send(origin, 0)

            @pl.when((at >= place) & (place > 0))
            def _():
                self.wait_send(origin, 1)


class SideFirstGather(SeqGather):
    def side(self):
        me_seq, me_head, outer, place, inner = seq_links()
        aside = other_of(me_seq)
        self.wait_arrival(aside)

        @pl.when(place < outer - 1)
        def _():
            self.send(aside, 0, (me_seq + 2, me_head))

        @pl.when(place > 0)
        def _():
            self.send(aside, 1, (me_seq - 2, me_head))

    def relay(self, step):
        me_seq, me_head, outer, place, inner = seq_links()
        below, above = me_seq - 2 * step, me_seq + 2 * step

        @pl.when(place >= step)
        def _():
            for origin in (below, other_of(below)):
                self.wait_arrival(origin)

                @pl.when(place < outer - 1)
                def _():
                    self.send(origin, 0, (me_seq + 2, me_head))

        @pl.when(place < outer - step)
        def _():
            for origin in (above, other_of(above)):
                self.wait_arrival(origin)

                @pl.when(place > 0)
                def _():
                    self.send(origin, 1, (me_seq - 2, me_head))

    def finish(self):
        me_seq, me_head, outer, place, inner = seq_links()
        self.local.wait()
        self.wait_send(me_seq, 2)
        for at in range(outer):
            for origin in (2 * at, 2 * at + 1):

                @pl.when((at <= place) & (place < outer - 1))
                def _():
                    self.wait_send(origin, 0)

                @pl.when((at >= place) & (place > 0))
                def _():
                    self.wait_send(origin, 1)


class HeadGather:
    def __init__(self, source, place_of, sends, receives):
        self.source, self.place_of = source, place_of
        self.sends, self.receives = sends, receives

    def links(self):
        me_seq, me_head = lax.axis_index("seq"), lax.axis_index("head")
        return me_seq, me_head, lax.axis_size("head") // 2

    def copy(self, origin, way, device, source=None):
        target = self.place_of(origin)
        return remote(
            target if source is None else source,
            target,
            self.sends.at[origin, way],
            self.receives.at[origin],
            device,
        )

    def start(self, local=None):
        me_seq, me_head, outer = self.links()
        self.local = None
        if local is not None:
            self.local = pltpu.make_async_copy(self.source, self.place_of(me_head), local)
            self.local.start()
        for step in range(1, outer):
            device = (me_seq, lax.rem(me_head + 2 * step, 2 * outer))
            self.copy(me_head, step, device, self.source).start()
        self.copy(me_head, 0, (me_seq, other_of(me_head)), self.source).start()

    def hand_on(self):
        me_seq, me_head, outer = self.links()
        for step in range(1, outer):
            origin = lax.rem(me_head + 2 * (outer - step), 2 * outer)
            self.copy(origin, 0, (me_seq, me_head)).wait_recv()
            self.copy(origin, 0, (me_seq, other_of(me_head))).start()

    def finish(self):
        me_seq, me_head, outer = self.links()
        if self.local is not None:
            self.local.wait()
        for step in range(outer):
            origin = lax.rem(other_of(me_head) + 2 * step, 2 * outer)
            self.copy(origin, 0, (me_seq, me_head)).wait_recv()
        for step in range(outer):
            origin = lax.rem(me_head + 2 * step, 2 * outer)
            self.copy(origin, 0, (me_seq, me_head)).wait_send()
        for step in range(1, outer):
            self.copy(me_head, step, (me_seq, me_head)).wait_send()


class HeadSum:
    def __init__(self, source, cores, rows, sends, receives):
        self.source, self.cores, self.rows = source, cores, rows
        self.sends, self.receives = sends, receives
        self.span = source.shape[1] // lax.axis_size("head")

    def links(self):
        me_seq, me_head = lax.axis_index("seq"), lax.axis_index("head")
        return me_seq, me_head, lax.axis_size("head") // 2

    def columns(self, origin):
        return pl.ds(pl.multiple_of(origin * self.span, self.span), self.span)

    def to_core(self, at):
        me_seq, me_head, outer = self.links()
        far = 2 * at + 1 - lax.rem(me_head, 2)
        return remote(
            self.source.at[self.rows, self.columns(far)],
            self.cores.at[at, self.rows, :],
            self.sends.at[at],
            self.receives.at[at],
            (me_seq, other_of(me_head)),
        )

    def start(self):
        for at in range(self.links()[2]):
            self.to_core(at).start()

    def add_core(self, at):
        me_seq, me_head, outer = self.links()
        self.to_core(at).wait()
        near = 2 * at + lax.rem(me_head, 2)
        mine = self.source[self.rows, self.columns(near)].astype(F32)
        total = mine + self.cores[at, self.rows, :].astype(F32)
        self.cores[at, self.rows, :] = total.astype(BF16)


def chunk_rows(chunk, size):
    return pl.ds(chunk * size, size)


FORWARD_IN = (
    ["lengths", "rate", "inputs", "cotangent", "gains", "conv", "w_small_t", "w_in", "w_out", "w_gate_t", "w_up_t", "w_down"]
)
FORWARD_OUT = ["rows", "grad_rows", "normed", "w_in_all", "proj", "logits", "table", "table_t", "w_small_all", "taps", "gain_one", "gain_heads", "query", "key", "value", "inverse", "solved", "ratio", "scores", "starts", "maps", "grad_mixed", "grad_gate_part", "residual", "gated", "branch", "normed_two", "inner", "grad_gate", "grad_up", "out_part", "hidden_own", "grad_hidden", "grad_gain_two", "grad_gain_heads", "residual_total", "pair", "aside"]


def forward_shapes(rows_here, model, block, heads, units, n_seq, n_head):
    groups = rows_here // GROUP
    unit = (heads, groups)
    span = model // n_head
    return dict(
        rows=((rows_here, model), BF16),
        grad_rows=((rows_here, model), BF16),
        normed=((rows_here + RIM, model), BF16),
        w_in_all=((model, block), BF16),
        proj=((rows_here + RIM, block), F32),
        logits=((8, rows_here), F32),
        table=((groups, TABLE_ROWS, MICRO), F32),
        table_t=((groups, MICRO, TABLE_ROWS), F32),
        w_small_all=((8, model), BF16),
        taps=((8, heads * (1 + 2 * HOUSE) * WIDTH), F32),
        gain_one=((1, model), F32),
        gain_heads=((1, heads * WIDTH), F32),
        query=(unit + (GROUP, WIDTH), F32),
        key=(unit + (MICRO, WIDTH), F32),
        value=(unit + (MICRO, WIDTH), F32),
        inverse=(unit + (MICRO, MICRO), BF16),
        solved=(unit + (MICRO, 2 * WIDTH), BF16),
        ratio=(unit + (MICRO, MICRO), F32),
        scores=(unit + (GROUP, MICRO), F32),
        starts=(unit + (WIDTH, WIDTH), BF16),
        maps=(unit + (WIDTH, WIDTH), BF16),
        grad_mixed=((rows_here, heads * WIDTH), F32),
        grad_gate_part=((rows_here, heads * WIDTH), BF16),
        residual=(unit + (WIDTH, WIDTH), F32),
        gated=((rows_here, heads * WIDTH), BF16),
        branch=((rows_here, model), BF16),
        normed_two=((rows_here, model), BF16),
        inner=((rows_here, units), BF16),
        grad_gate=((rows_here, units), BF16),
        grad_up=((rows_here, units), BF16),
        out_part=((rows_here, model), BF16),
        hidden_own=((rows_here, span), F32),
        grad_hidden=((rows_here, span), F32),
        grad_gain_two=((1, span), F32),
        grad_gain_heads=((1, heads * WIDTH), F32),
        residual_total=((heads, WIDTH, WIDTH), F32),
        pair=((heads, WIDTH, 2 * WIDTH), F32),
        aside=((heads, WIDTH, 2 * WIDTH), F32),
    )


def spread_lanes(blocks, width, total):
    found = None
    for at, block in enumerate(blocks):
        place = rows_of(block.shape[1]) + at * width == lanes_of(total)
        place = place & (rows_of(block.shape[1]) < width)
        part = dot(block.astype(BF16), place.astype(BF16))
        found = part if found is None else found + part
    return found


def forward_kernel(names, sizes, *refs):
    r = SimpleNamespace(**dict(zip(names, refs)))
    rows_here, model, block, heads, units, n_seq, n_head = sizes
    groups = rows_here // GROUP
    outer_head = n_head // 2
    span = model // n_head
    depth = model // n_seq
    channels = (1 + 2 * HOUSE) * WIDTH
    head_block = block // heads
    me_seq, me_head, outer, place, inner = seq_links()
    core = lax.rem(me_head, 2)
    first = me_seq * rows_here
    bounds = bounds_of(r.lengths)
    after = (lax.rem(me_seq + 1, n_seq), me_head)
    before = (lax.rem(me_seq + n_seq - 1, n_seq), me_head)

    r.tile[...] = jnp.zeros_like(r.tile)
    gain_span, conv_span = r.gains.shape[1], r.conv.shape[1]
    r.tile[0:3, 0:gain_span] = r.gains[...]
    r.tile[4:8, 0:conv_span] = r.conv[...].astype(F32)
    r.tile[8 : 8 + r.w_small_t.shape[0], 0:depth] = r.w_small_t[...].astype(F32)
    greet(seq_neighbours() + head_neighbours() + [(None, after), (None, before)])

    def part_of(target):
        return lambda origin: target.at[:, pl.ds(pl.multiple_of(origin * span, span), span)]

    def rows_at(target, lanes=None):
        lanes = slice(None) if lanes is None else lanes
        return lambda origin: target.at[pl.ds(pl.multiple_of(origin * depth, depth), depth), lanes]

    take_rows = HeadGather(r.inputs, part_of(r.rows), r.head_sends.at[0], r.head_receives.at[0])
    take_grad = HeadGather(
        r.cotangent, part_of(r.grad_rows), r.head_sends.at[1], r.head_receives.at[1]
    )
    take_tile = SeqGather(
        r.tile, lambda origin: r.tiles.at[origin], r.seq_sends.at[0], r.seq_receives.at[0]
    )
    seq_gather = lambda at, kind, source, target: kind(
        source, rows_at(target), r.seq_sends.at[at], r.seq_receives.at[at]
    )
    take_out = seq_gather(1, SeqGather, r.out_shard, r.w_out_own)
    take_down = seq_gather(2, SideFirstGather, r.down_shard, r.down_all)
    take_gate = seq_gather(3, SeqGather, r.gate_shard, r.gate_all)
    take_up = seq_gather(4, SeqGather, r.up_shard, r.up_all)
    take_units = [take_down, take_gate, take_up]
    take_in = []
    for head in range(heads):
        lanes = pl.ds(head * head_block, head_block)
        take_in.append(
            SeqGather(
                r.w_in.at[:, lanes],
                rows_at(r.w_in_all, lanes),
                r.seq_sends.at[5 + head],
                r.seq_receives.at[5 + head],
            )
        )
    first_in, last_in = take_in[0], take_in[-1]
    take_tile.start(r.local.at[2])
    take_rows.start(r.local.at[0])
    first_in.start(r.local.at[7])
    take_grad.start(r.local.at[1])
    r.masks[...] = jnp.stack([mask.astype(F32) for mask in level_masks()]).astype(BF16)
    r.out_shard[...] = jnp.transpose(r.w_out[...])
    r.down_shard[...] = jnp.transpose(r.w_down[...])
    take_rows.hand_on()
    take_rows.finish()
    tail = r.rows.at[pl.ds(rows_here - RIM, RIM), :]
    rim_copy = remote(tail, r.rim, r.rim_sems.at[0], r.rim_sems.at[1], after)
    rim_copy.start()
    take_tile.advance()
    first_in.advance()
    for head in range(1, heads):
        take_in[head].start(r.local.at[7 + head])
    take_tile.drain()
    take_tile.finish()
    wide_tile = HeadGather(
        r.tiles.at[:, pl.ds(0, 8), :],
        lambda origin: r.wide_tiles.at[origin],
        r.head_sends.at[2],
        r.head_receives.at[2],
    )
    wide_tile.start(r.local.at[3])
    r.gate_shard[...] = jnp.transpose(r.w_gate_t[...])
    r.up_shard[...] = jnp.transpose(r.w_up_t[...])
    first_in.advance()
    if heads > 1:
        last_in.advance()
    take_out.start(r.local.at[4])
    take_grad.hand_on()
    wide_tile.hand_on()
    wide_tile.finish()
    gains = spread_lanes(
        [r.wide_tiles[head, seq] for head in range(n_head) for seq in range(n_seq)],
        gain_span,
        model,
    )
    r.gain_one[...] = gains[0:1]
    r.gain_two[...] = gains[1:2]
    own_gains = spread_lanes(
        [r.tiles[seq][0:8] for seq in range(n_seq)], gain_span, heads * WIDTH
    )
    r.gain_heads[...] = own_gains[2:3]
    taps = spread_lanes([r.tiles[seq][0:8] for seq in range(n_seq)], conv_span, heads * channels)
    r.taps[0:4, :] = taps[4:8]
    r.taps[4:8, :] = jnp.zeros((4, heads * channels), F32)
    small = spread_lanes([r.tiles[seq][8:16] for seq in range(n_seq)], depth, model)
    r.w_small_all[...] = small.astype(BF16)
    rim_copy.wait()

    def normed_of(values):
        values = values.astype(F32)
        scale = lax.rsqrt(row_sum(values * values) / model + EPSILON)
        return (values * scale * r.gain_one[...]).astype(BF16)

    r.normed[0:RIM, :] = normed_of(jnp.where(me_seq > 0, r.rim[...].astype(F32), 0.0))
    tile = min(256, rows_here)

    @pl.loop(0, rows_here // tile)
    def _(at):
        rows = pl.ds(pl.multiple_of(at * tile, tile), tile)
        shifted = pl.ds(pl.multiple_of(at * tile + RIM, RIM), tile)
        r.normed[shifted, :] = normed_of(r.rows[rows, :])

    r.logits[...] = dot(r.w_small_all[...], r.normed[RIM:, :], (1, 1))
    rates = [r.rate[head] for head in range(heads)]
    fill_tables(r.logits[...], rates, heads, groups, first, bounds, r.table, r.table_t)
    first_in.drain()
    if heads > 1:
        last_in.advance()
    take_out.advance()

    pair = 2 * depth
    pieces = pair % WIDTH == 0

    def project(head, at, fresh):
        columns = pl.ds(head * head_block, head_block)
        if pieces:
            lanes = pl.ds(pl.multiple_of(at * pair, pair), pair)
            weights = pl.ds(pl.multiple_of(at * pair, pair), pair)
        else:
            lanes = weights = slice(None)

        def one(rows):
            part = dot(r.normed[rows, lanes], r.w_in_all[weights, columns])
            r.proj[rows, columns] = part if fresh else r.proj[rows, columns] + part

        one(pl.ds(0, RIM))

        @pl.loop(0, rows_here // tile)
        def _(turn):
            one(pl.ds(pl.multiple_of(turn * tile + RIM, RIM), tile))

    def project_head(head):
        gather = take_in[head]
        gather.drain()
        gather.local.wait()
        if pieces:
            gather.wait_arrival(other_of(me_seq))
            project(head, place, True)
            for step in range(1, outer):

                @pl.when(place >= step)
                def _():
                    gather.wait_arrival(other_of(me_seq) - 2 * step)
                    project(head, place - step, False)

                @pl.when(place < outer - step)
                def _():
                    gather.wait_arrival(other_of(me_seq) + 2 * step)
                    project(head, place + step, False)

        gather.finish(False, not pieces)
        if not pieces:
            project(head, 0, True)

    saves = []

    def save(name, source=None):
        source = getattr(r, name) if source is None else source
        copy = pltpu.make_async_copy(source, getattr(r, "out_" + name), r.saved.at[len(saves)])
        copy.start()
        saves.append(copy)

    eye = (rows_of(MICRO) == lanes_of(MICRO)).astype(F32)
    strict = micro_order(lanes_of(MICRO)) < micro_order(rows_of(MICRO))
    zero = jnp.zeros((WIDTH, WIDTH), F32)
    together = min(4, groups)

    def chain(head, slot):
        so_far = r.total[head]
        r.before[head, slot] = so_far
        joined = dot_mid(r.chain_map[head, slot], so_far)
        added = jnp.concatenate([zero, r.chain_add[head, slot]], axis=1)
        r.total[head] = joined + added

    def mix_head(head):
        r.total[head] = jnp.concatenate([eye, zero], axis=1)
        for at in range(together):
            r.chain_map[head, at] = eye
            r.chain_add[head, at] = zero

        @pl.loop(0, groups // together)
        def _(turn):
            for extra in range(together):
                chain(head, turn * together + extra)
            found = []
            for extra in range(together):
                group = turn * together + extra
                columns, keeps = group_columns(r.table_t, group, heads)
                table = r.table[group]
                reach = reach_of(columns, table)
                parts = []
                for part in range(1 + 2 * HOUSE):
                    taps_at = head * channels + part * WIDTH
                    window = conv_window(r.proj, group, head * head_block + part * WIDTH)
                    total = conv_total(window, keeps, r.taps[:, taps_at : taps_at + WIDTH])
                    mixed = total * jax.nn.sigmoid(total)
                    if part < 1 + HOUSE:
                        mixed = mixed * lax.rsqrt(row_sum(mixed * mixed) + EPSILON)
                    parts.append(mixed)
                query = parts[0]
                keys = jnp.concatenate(parts[1 : 1 + HOUSE], axis=0)
                values = jnp.concatenate(parts[1 + HOUSE :], axis=0)
                beta, growth, to_end = (
                    columns[:, 4 * head + at : 4 * head + at + 1] for at in (0, 2, 3)
                )
                decay = decay_of(columns, table, head, reach)
                both = dot_mid(jnp.concatenate([keys, query], axis=0), keys, (1, 1))
                ratio = jnp.where(strict, decay * both[:MICRO], 0.0)
                scores = decay[GROUP:] * both[MICRO:]
                r.query[head, group] = query
                r.key[head, group] = keys
                r.value[head, group] = values
                r.ratio[head, group] = ratio
                r.scores[head, group] = scores
                found.append(
                    (group, query, keys, values, beta, growth, to_end, scores, ratio * beta)
                )
            inverses = unit_inverse([unit[-1] for unit in found], r.masks)
            for unit, inverse in zip(found, inverses):
                group, query, keys, values, beta, growth, to_end, scores, lower = unit
                right = jnp.concatenate([beta * values, (beta * growth) * keys], axis=1)
                solved = dot_mid(inverse, right)
                seen = dot_mid(scores, solved)
                carried = dot_mid(to_end * keys, solved, (0, 0))
                r.inverse[head, group] = inverse.astype(BF16)
                r.solved[head, group] = solved.astype(BF16)
                r.local_out[head, group] = seen[:, :WIDTH]
                r.reach[head, group] = growth[GROUP:] * query - seen[:, WIDTH:]
                slot = group + together
                map_here = growth[MICRO - 1 : MICRO] * eye - carried[:, WIDTH:]
                r.chain_map[head, slot] = map_here
                r.maps[head, group] = map_here.astype(BF16)
                r.chain_add[head, slot] = carried[:, :WIDTH]

        for extra in range(together):
            chain(head, groups + extra)

    project_head(0)
    if heads > 1:
        last_in.drain()
    take_out.advance()
    for at, gather in enumerate(take_units):
        gather.start(r.local.at[7 + heads + at])
    for name in ["rows", "normed", "logits", "w_small_all", "taps", "gain_one", "gain_heads", "table", "table_t"]:
        save(name)
    mix_head(0)
    take_out.drain()
    take_down.side()
    for head in range(1, heads):
        project_head(head)
    save("proj")
    save("w_in_all")
    take_out.finish()
    wide_out = HeadGather(
        r.w_out_own,
        lambda origin: r.w_out_all.at[origin],
        r.head_sends.at[3],
        r.head_receives.at[3],
    )
    wide_out.start(r.local.at[5])
    for head in range(1, heads):
        mix_head(head)

    r.own[...] = r.total[...].astype(BF16)
    swap = remote(r.own, r.theirs, r.swap.at[0], r.swap.at[1], (other_of(me_seq), me_head))
    swap.start()
    for name in ["query", "key", "value", "inverse", "solved", "ratio", "scores", "maps"]:
        save(name)
    for gather in take_units:
        gather.advance()
    wide_out.hand_on()
    swap.wait()
    for head in range(heads):
        mine, other = r.own[head].astype(F32), r.theirs[head].astype(F32)
        r.aside[head] = other
        early = jnp.where(inner == 0, mine, other)
        late = jnp.where(inner == 0, other, mine)
        joined = dot_mid(late[:, :WIDTH], early)
        r.pair[head] = joined + jnp.concatenate([zero, late[:, WIDTH:]], axis=1)
    step_up = remote(r.moving, r.arriving, r.swap.at[2], r.swap.at[3], (me_seq + 2, me_head))

    def relay_state():
        @pl.when(place > 0)
        def _():
            step_up.wait_recv()

        for head in range(heads):
            state = jnp.where(place > 0, r.arriving[head].astype(F32), 0.0)
            moved = dot_mid(r.pair[head, :, :WIDTH], state) + r.pair[head, :, WIDTH:]
            r.moving[head] = moved.astype(BF16)

        @pl.when(place < outer - 1)
        def _():
            step_up.start()

        for head in range(heads):
            state = jnp.where(place > 0, r.arriving[head].astype(F32), 0.0)
            stepped = dot_mid(r.aside[head, :, :WIDTH], state) + r.aside[head, :, WIDTH:]
            r.state[head] = jnp.where(inner == 0, state, stepped)
            r.pair[head, :, WIDTH:] = r.own[head, :, :WIDTH].astype(F32)

    pl.when(place < 3)(relay_state)
    take_grad.finish()
    for gather in take_units:
        gather.advance()
    pl.when(place >= 3)(relay_state)
    for name in ["pair", "aside", "grad_rows"]:
        save(name)

    size = min(256, rows_here)
    chunks = rows_here // size
    order = list(reversed(range(chunks)))
    per_chunk = size // GROUP
    r.grad_gain_two[...] = jnp.zeros_like(r.grad_gain_two)
    r.grad_gain_heads[...] = jnp.zeros_like(r.grad_gain_heads)
    for head in range(heads):
        r.residual_total[head] = zero

    def gated_gather(chunk):
        rows = chunk_rows(chunk, size)
        return HeadGather(
            r.gated.at[rows, :],
            lambda origin: r.gated_rows.at[
                rows, pl.ds(pl.multiple_of(origin * span, span), span)
            ],
            r.gated_sends.at[chunk],
            r.gated_receives.at[chunk],
        )

    gathers = {}

    def mix(chunk):
        @pl.loop(chunk * per_chunk, (chunk + 1) * per_chunk)
        def _(group):
            rows = pl.ds(pl.multiple_of(group * GROUP, GROUP), GROUP)
            shifted = pl.ds(pl.multiple_of(group * GROUP + RIM, RIM), GROUP)
            for head in range(heads):
                so_far = r.before[head, group + together]
                start = dot_mid(so_far[:, :WIDTH], r.state[head]) + so_far[:, WIDTH:]
                r.starts[head, group] = start.astype(BF16)
                out = r.local_out[head, group] + dot_mid(r.reach[head, group], start)
                lanes = slice(head * WIDTH, (head + 1) * WIDTH)
                r.mixed[rows, lanes] = out
                scale = lax.rsqrt(row_sum(out * out) / WIDTH + EPSILON)
                at = (head + 1) * head_block - WIDTH
                gate = r.proj[shifted, at : at + WIDTH]
                gated = out * scale * r.gain_heads[:, lanes] * (gate * jax.nn.sigmoid(gate))
                r.gated[rows, lanes] = gated.astype(BF16)

        gathers[chunk] = gated_gather(chunk)
        gathers[chunk].start(r.gated_local.at[chunk])

    def back_sum(chunk):
        return HeadSum(
            r.back,
            r.cores,
            chunk_rows(chunk, size),
            r.core_sends.at[chunk],
            r.core_receives.at[chunk],
        )

    def to_chip(chunk, step):
        rows = chunk_rows(chunk, size)
        return remote(
            r.cores.at[:, rows, :],
            r.chips.at[step, :, rows, :],
            r.chip_sends.at[chunk, step],
            r.chip_receives.at[chunk, step],
            (me_seq, lax.rem(me_head + 2 * step, n_head)),
        )

    def columns_of(origin):
        return pl.ds(pl.multiple_of(origin * span, span), span)

    def to_total(chunk, at):
        near = r.summed.at[chunk_rows(chunk, size), columns_of(2 * at + core)]
        return remote(
            near,
            near,
            r.last_sends.at[chunk, at],
            r.last_receives.at[chunk, at],
            (me_seq, other_of(me_head)),
        )

    def hidden_rows(chunk):
        gathers[chunk].hand_on()
        gathers[chunk].finish()
        rows = chunk_rows(chunk, size)
        hidden = r.rows[rows, :].astype(F32)
        for head in range(n_head):
            part = r.gated_rows[rows, head * span : (head + 1) * span]
            hidden = hidden + dot(part, r.w_out_all[head], (1, 1))
        r.hidden[rows, :] = hidden
        scale = lax.rsqrt(row_sum(hidden * hidden) / model + EPSILON)
        r.normed_two[rows, :] = (hidden * scale * r.gain_two[...]).astype(BF16)

    def feed_forward(chunk):
        rows = chunk_rows(chunk, size)
        normed = r.normed_two[rows, :]
        grad_inner = dot(r.grad_rows[rows, :], r.down_all[...])
        gate = dot(normed, r.gate_all[...])
        up = dot(normed, r.up_all[...])
        sigma = jax.nn.sigmoid(gate)
        swish = gate * sigma
        inner_here = (swish * up).astype(BF16)
        r.inner[rows, :] = inner_here
        grad_gate = (grad_inner * up * sigma * (1.0 + gate * (1.0 - sigma))).astype(BF16)
        grad_up = (grad_inner * swish).astype(BF16)
        r.grad_gate[rows, :] = grad_gate
        r.grad_up[rows, :] = grad_up
        back = dot(grad_gate, r.gate_all[...], (1, 1)) + dot(grad_up, r.up_all[...], (1, 1))
        r.back[rows, :] = back.astype(BF16)
        back_sum(chunk).start()
        r.out_part[rows, :] = dot(inner_here, r.down_all[...], (1, 1)).astype(BF16)

    def add_cores(chunk):
        for at in range(outer_head):
            back_sum(chunk).add_core(at)
        for step in range(1, outer_head):
            to_chip(chunk, step).start()

    def add_chips(chunk):
        for step in range(1, outer_head):
            to_chip(chunk, step).wait()
        rows = chunk_rows(chunk, size)
        for at in range(outer_head):
            value = r.cores[at, rows, :].astype(F32)
            for step in range(1, outer_head):
                value = value + r.chips[step, at, rows, :].astype(F32)
            r.summed[rows, columns_of(2 * at + core)] = value.astype(BF16)
            to_total(chunk, at).start()

    def norm_back(chunk):
        for at in range(outer_head):
            to_total(chunk, at).wait()
        rows = chunk_rows(chunk, size)
        own = columns_of(me_head)
        hidden = r.hidden[rows, :]
        scale = lax.rsqrt(row_sum(hidden * hidden) / model + EPSILON)
        weighted = r.summed[rows, :].astype(F32) * r.gain_two[...]
        pull = scale * scale * scale * (row_sum(weighted * hidden) / model)
        grad = scale * weighted - hidden * pull + r.grad_rows[rows, :].astype(F32)
        branch = grad.astype(BF16)
        r.branch[rows, :] = branch
        hidden_own = r.hidden[rows, own]
        back_own = r.summed[rows, own].astype(F32)
        r.hidden_own[rows, :] = hidden_own
        grad_own = scale * back_own * r.gain_two[:, own] - hidden_own * pull
        r.grad_hidden[rows, :] = grad_own + r.grad_rows[rows, own].astype(F32)
        r.grad_gain_two[...] += jnp.sum(back_own * hidden_own * scale, axis=0, keepdims=True)
        grad_gated = dot(branch, r.w_out_own[...])
        shifted = pl.ds(chunk * size + RIM, size)
        for head in range(heads):
            lanes = slice(head * WIDTH, (head + 1) * WIDTH)
            gain = r.gain_heads[:, lanes]
            out = r.mixed[rows, lanes]
            scale_out = lax.rsqrt(row_sum(out * out) / WIDTH + EPSILON)
            at = (head + 1) * head_block - WIDTH
            gate = r.proj[shifted, at : at + WIDTH]
            sigma = jax.nn.sigmoid(gate)
            grad_here = grad_gated[:, lanes]
            scaled = out * scale_out
            grad_normed = grad_here * gate * sigma
            slope = sigma * (1.0 + gate * (1.0 - sigma))
            r.grad_gate_part[rows, lanes] = (grad_here * scaled * gain * slope).astype(BF16)
            r.grad_gain_heads[:, lanes] += jnp.sum(grad_normed * scaled, axis=0, keepdims=True)
            weighted_out = grad_normed * gain
            mean = row_sum(weighted_out * scaled) / WIDTH
            r.grad_mixed[rows, lanes] = scale_out * (weighted_out - scaled * mean)
        for turn in range(per_chunk):
            group = (chunk + 1) * per_chunk - 1 - turn
            for head in range(heads):
                grad_out = r.grad_mixed[
                    group * GROUP : (group + 1) * GROUP, head * WIDTH : (head + 1) * WIDTH
                ]
                residual = dot_low(r.reach[head, group], grad_out, (0, 0))
                r.residual[head, group] = residual
                r.residual_total[head] = residual + dot(
                    r.maps[head, group], r.residual_total[head].astype(BF16), (0, 0)
                )

    for chunk in order:
        mix(chunk)
    wide_out.finish()
    for chunk in order:
        hidden_rows(chunk)
    for gather in take_units:
        gather.drain()
        gather.finish()
    for at, chunk in enumerate(order):
        feed_forward(chunk)
        add_cores(chunk)
        if at > 0:
            add_chips(order[at - 1])
            norm_back(order[at - 1])
    add_chips(order[-1])
    for name in ["starts", "gated", "normed_two", "inner", "grad_gate", "grad_up", "out_part"]:
        save(name)
    norm_back(order[-1])
    for name in ["grad_mixed", "grad_gate_part", "residual", "branch", "hidden_own", "grad_hidden", "grad_gain_two", "grad_gain_heads", "residual_total"]:
        save(name)

    @pl.when(place < outer - 1)
    def _():
        step_up.wait_send()

    for copy in saves:
        copy.wait()


def forward_call(arguments, sizes):
    rows_here, model, block, heads, units, n_seq, n_head = sizes
    groups = rows_here // GROUP
    unit = (heads, groups)
    depth, span = model // n_seq, model // n_head
    outer_head = n_head // 2
    kept = forward_shapes(*sizes)
    named = dict(zip(FORWARD_IN, arguments))
    tile_lanes = max(named["conv"].shape[1], depth, WIDTH)
    tile_lanes = -(-tile_lanes // WIDTH) * WIDTH
    size = min(256, rows_here)
    chunks = rows_here // size
    together = min(4, groups)
    own = heads * WIDTH
    vmem = lambda dims, kind=F32: pltpu.VMEM(dims, kind)
    scratch = {name: vmem(*kept[name]) for name in FORWARD_OUT}
    scratch.update(
        gate_shard=vmem((depth, units), BF16),
        up_shard=vmem((depth, units), BF16),
        down_shard=vmem((depth, units), BF16),
        out_shard=vmem((depth, own), BF16),
        tile=vmem((16, tile_lanes)),
        tiles=vmem((n_seq, 16, tile_lanes)),
        wide_tiles=vmem((n_head, n_seq, 8, tile_lanes)),
        rim=vmem((RIM, model), BF16),
        gain_two=vmem((1, model)),
        masks=vmem((7, MICRO, MICRO), BF16),
        w_out_own=vmem((model, own), BF16),
        w_out_all=vmem((n_head, model, own), BF16),
        gate_all=vmem((model, units), BF16),
        up_all=vmem((model, units), BF16),
        down_all=vmem((model, units), BF16),
        total=vmem((heads, WIDTH, 2 * WIDTH)),
        chain_map=vmem((heads, groups + together, WIDTH, WIDTH)),
        chain_add=vmem((heads, groups + together, WIDTH, WIDTH)),
        before=vmem((heads, groups + together, WIDTH, 2 * WIDTH)),
        local_out=vmem(unit + (GROUP, WIDTH)),
        reach=vmem(unit + (GROUP, WIDTH)),
        own=vmem((heads, WIDTH, 2 * WIDTH), BF16),
        theirs=vmem((heads, WIDTH, 2 * WIDTH), BF16),
        moving=vmem((heads, WIDTH, WIDTH), BF16),
        arriving=vmem((heads, WIDTH, WIDTH), BF16),
        state=vmem((heads, WIDTH, WIDTH)),
        mixed=vmem((rows_here, own)),
        gated_rows=vmem((rows_here, model), BF16),
        hidden=vmem((rows_here, model)),
        back=vmem((rows_here, model), BF16),
        summed=vmem((rows_here, model), BF16),
        cores=vmem((outer_head, rows_here, span), BF16),
        chips=vmem((outer_head, outer_head, rows_here, span), BF16),
        head_sends=DMA((4, n_head, outer_head)),
        head_receives=DMA((4, n_head)),
        local=DMA((10 + heads,)),
        rim_sems=DMA((2,)),
        seq_sends=DMA((5 + heads, n_seq, 3)),
        seq_receives=DMA((5 + heads, n_seq)),
        swap=DMA((4,)),
        gated_sends=DMA((chunks, n_head, outer_head)),
        gated_receives=DMA((chunks, n_head)),
        gated_local=DMA((chunks,)),
        core_sends=DMA((chunks, outer_head)),
        core_receives=DMA((chunks, outer_head)),
        chip_sends=DMA((chunks, outer_head)),
        chip_receives=DMA((chunks, outer_head)),
        last_sends=DMA((chunks, outer_head)),
        last_receives=DMA((chunks, outer_head)),
        saved=DMA((len(FORWARD_OUT),)),
    )
    names = FORWARD_IN + ["out_" + name for name in FORWARD_OUT] + list(scratch)
    outs = pl.pallas_call(
        partial(forward_kernel, names, sizes),
        out_shape=[shape(*kept[name]) for name in FORWARD_OUT],
        in_specs=[SMEM, SMEM, ANY, ANY, VMEM, VMEM, VMEM, ANY, VMEM, VMEM, VMEM, VMEM],
        out_specs=[ANY] * len(FORWARD_OUT),
        scratch_shapes=list(scratch.values()),
        compiler_params=pltpu.CompilerParams(
            collective_id=0, has_side_effects=True, vmem_limit_bytes=VMEM_BYTES
        ),
        name="forward",
    )(*arguments)
    return SimpleNamespace(**dict(zip(FORWARD_OUT, outs)))


def far_order(outer):
    return sorted(range(outer), key=lambda far: -abs(2 * far + 1 - outer))


class SeqSum:
    def __init__(self, partial_ref, sides, ups, downs, sends, receives):
        self.partial, self.sides, self.ups, self.downs = partial_ref, sides, ups, downs
        self.sends, self.receives = sends, receives
        self.depth = sides.shape[1]
        self.next = 1

    def rows_for(self, dest):
        return pl.ds(pl.multiple_of(dest * self.depth, self.depth), self.depth)

    def to_side(self, far):
        me_seq, me_head, outer, place, inner = seq_links()
        return remote(
            self.partial.at[self.rows_for(2 * far + 1 - inner), :],
            self.sides.at[far],
            self.sends.at[0, far],
            self.receives.at[0, far],
            (other_of(me_seq), me_head),
        )

    def along(self, way, far):
        me_seq, me_head, outer, place, inner = seq_links()
        return remote(
            self.sides.at[far],
            (self.ups if way == 1 else self.downs).at[far],
            self.sends.at[way, far],
            self.receives.at[way, far],
            (me_seq + 2 if way == 1 else me_seq - 2, me_head),
        )

    def send_sides(self):
        for far in far_order(lax.axis_size("seq") // 2):
            self.to_side(far).start()

    def tiles(self, body):
        tile = min(self.depth, 32)

        @pl.loop(0, self.depth // tile)
        def _(turn):
            body(pl.ds(pl.multiple_of(turn * tile, tile), tile), turn * tile, tile)

    def add_sides(self):
        me_seq, me_head, outer, place, inner = seq_links()
        for far in far_order(outer):
            self.to_side(far).wait_recv()

            def body(rows, start, tile, far=far):
                at = pl.multiple_of((2 * far + inner) * self.depth + start, tile)
                mine = self.partial[pl.ds(at, tile), :].astype(F32)
                total = mine + self.sides[far, rows, :].astype(F32)
                self.sides[far, rows, :] = total.astype(self.sides.dtype)

            self.tiles(body)

            @pl.when((place == 0) & (far > 0))
            def _():
                self.along(1, far).start()

            @pl.when((place == outer - 1) & (far < outer - 1))
            def _():
                self.along(2, far).start()

    def pass_on(self, way, far):
        came = self.ups if way == 1 else self.downs
        self.along(way, far).wait_recv()

        def body(rows, start, tile):
            total = self.sides[far, rows, :].astype(F32) + came[far, rows, :].astype(F32)
            self.sides[far, rows, :] = total.astype(self.sides.dtype)

        self.tiles(body)
        self.along(way, far).start()

    def advance(self):
        me_seq, me_head, outer, place, inner = seq_links()
        if self.next > outer - 2:
            return
        step = self.next
        self.next += 1

        @pl.when(place == step)
        def _():
            for far in reversed(range(step + 1, outer)):
                self.pass_on(1, far)

        @pl.when(place == outer - 1 - step)
        def _():
            for far in range(0, outer - 1 - step):
                self.pass_on(2, far)

    def result(self, target):
        me_seq, me_head, outer, place, inner = seq_links()
        while self.next <= outer - 2:
            self.advance()

        def fill(terms):
            def body(rows, start, tile):
                total = self.sides[place, rows, :].astype(F32)
                for term in terms:
                    total = total + term[place, rows, :].astype(F32)
                target[rows, :] = total

            self.tiles(body)

        @pl.when(place > 0)
        def _():
            self.along(1, place).wait_recv()

        @pl.when(place < outer - 1)
        def _():
            self.along(2, place).wait_recv()

        @pl.when(place == 0)
        def _():
            fill([self.downs])

        @pl.when(place == outer - 1)
        def _():
            fill([self.ups])

        @pl.when((place > 0) & (place < outer - 1))
        def _():
            fill([self.ups, self.downs])

    def finish(self):
        me_seq, me_head, outer, place, inner = seq_links()
        for far in range(outer):
            self.to_side(far).wait_send()

            @pl.when(far > place)
            def _():
                self.along(1, far).wait_send()

            @pl.when(far < place)
            def _():
                self.along(2, far).wait_send()


BACK_IN = ["rows", "grad_rows", "normed", "w_in_all", "proj", "logits", "table", "table_t", "w_small_all", "taps", "gain_one", "query", "key", "value", "inverse", "solved", "ratio", "scores", "starts", "maps", "grad_mixed", "grad_gate_part", "residual", "gated", "branch", "normed_two", "inner", "grad_gate", "grad_up", "out_part", "hidden_own", "grad_hidden", "grad_gain_two", "grad_gain_heads", "residual_total", "pair", "aside"]
BACK_OUT = ["result", "grad_inputs", "grad_w_in", "grad_w_gate_t", "grad_w_up_t", "grad_w_down", "grad_w_out", "small_sums"]


def back_kernel(names, sizes, *refs):
    r = SimpleNamespace(**dict(zip(names, refs)))
    rows_here, model, block, heads, units, n_seq, n_head = sizes
    groups = rows_here // GROUP
    outer_head = n_head // 2
    span = model // n_head
    depth = model // n_seq
    channels = (1 + 2 * HOUSE) * WIDTH
    head_block = block // heads
    me_seq, me_head, outer, place, inner = seq_links()
    chip = me_head // 2
    after = (lax.rem(me_seq + 1, n_seq), me_head)
    before = (lax.rem(me_seq + n_seq - 1, n_seq), me_head)
    greet(seq_neighbours() + head_neighbours() + [(None, after), (None, before)])

    loads = {}
    for name in ["residual_total", "pair", "aside", "grad_rows", "inner", "normed_two", "grad_gate", "grad_up", "branch", "gated", "out_part", "hidden_own", "maps", "residual", "table", "table_t", "taps", "query", "key", "value", "inverse", "solved", "ratio", "scores", "starts", "grad_mixed", "proj", "grad_gate_part", "normed", "logits", "w_small_all", "gain_one", "w_in_all", "rows", "grad_hidden", "grad_gain_two", "grad_gain_heads"]:
        source = getattr(r, "in_" + name)
        loads[name] = pltpu.make_async_copy(source, getattr(r, name), r.loaded.at[len(loads)])
        loads[name].start()

    def need(*words):
        for name in words:
            if name in loads:
                loads.pop(name).wait()

    need("residual_total", "pair", "aside")
    r.own[...] = r.residual_total[...].astype(BF16)
    swap = remote(r.own, r.theirs, r.swap.at[0], r.swap.at[1], (other_of(me_seq), me_head))
    swap.start()

    part_of = {}
    for at, name in enumerate(["down", "gate", "up", "out"]):
        part_of[name] = SeqSum(
            getattr(r, "sum_" + name),
            getattr(r, "sides_" + name),
            getattr(r, "ups_" + name),
            getattr(r, "downs_" + name),
            r.sum_sends.at[at],
            r.sum_receives.at[at],
        )

    def weight_grad(name, left, right):
        pair = 2 * depth
        for far in far_order(outer):
            lanes = slice(far * pair, (far + 1) * pair)
            found = dot(left[:, lanes], right[...], (0, 0))
            getattr(r, "sum_" + name)[lanes, :] = found.astype(BF16)
            part_of[name].to_side(far).start()

    step_down = remote(r.moving, r.arriving, r.swap.at[2], r.swap.at[3], (me_seq - 2, me_head))

    def relay_adjoint():
        @pl.when(place < outer - 1)
        def _():
            step_down.wait_recv()

        for head in range(heads):
            mine, other = r.own[head].astype(F32), r.theirs[head].astype(F32)
            adjoint = jnp.where(place < outer - 1, r.arriving[head].astype(F32), 0.0)
            late = jnp.where(inner == 0, other, mine)
            early = jnp.where(inner == 0, mine, other)
            map_other = r.aside[head, :, :WIDTH]
            early_map = jnp.where(inner == 0, r.pair[head, :, WIDTH:], map_other)
            joined = early + dot_mid(early_map, late, (0, 0))
            moved = joined + dot_mid(r.pair[head, :, :WIDTH], adjoint, (0, 0))
            r.moving[head] = moved.astype(BF16)

        @pl.when(place > 0)
        def _():
            step_down.start()

        for head in range(heads):
            mine, other = r.own[head].astype(F32), r.theirs[head].astype(F32)
            adjoint = jnp.where(place < outer - 1, r.arriving[head].astype(F32), 0.0)
            late = jnp.where(inner == 0, other, mine)
            stepped = late + dot_mid(r.aside[head, :, :WIDTH], adjoint, (0, 0))
            r.running[head] = jnp.where(inner == 0, stepped, adjoint)

    need("grad_rows", "inner")
    weight_grad("down", r.grad_rows, r.inner)
    swap.wait()
    pl.when(place == outer - 1)(relay_adjoint)
    need("normed_two", "grad_gate")
    weight_grad("gate", r.normed_two, r.grad_gate)
    pl.when(place == outer - 2)(relay_adjoint)
    need("grad_up")
    weight_grad("up", r.normed_two, r.grad_up)
    pl.when(place == outer - 3)(relay_adjoint)
    need("branch", "gated", "out_part", "hidden_own")
    weight_grad("out", r.branch, r.gated)

    whole = pl.ds(0, rows_here)
    out_sum = HeadSum(r.out_part, r.out_cores, whole, r.core_sends.at[0], r.core_receives.at[0])
    back_sum = HeadSum(r.back_one, r.back_cores, whole, r.core_sends.at[1], r.core_receives.at[1])

    def to_chip(at, cores, chips, step):
        target = lax.rem(me_head + 2 * step, n_head)
        return remote(
            cores.at[target // 2],
            chips.at[step],
            r.chip_sends.at[at, step],
            r.chip_receives.at[at, step],
            (me_seq, target),
        )

    out_sum.start()
    pl.when(place < outer - 3)(relay_adjoint)

    need("maps", "residual")

    @pl.loop(0, groups)
    def _(turn):
        group = groups - 1 - turn
        for head in range(heads):
            here = r.running[head]
            r.leaving[head, group] = here.astype(BF16)
            r.running[head] = r.residual[head, group] + dot(
                r.maps[head, group], here.astype(BF16), (0, 0)
            )

    need("table", "table_t", "taps", "query", "key", "value", "inverse", "solved", "ratio", "scores", "starts", "grad_mixed", "proj")
    r.grad_conv[...] = jnp.zeros_like(r.grad_conv)
    r.grad_taps[...] = jnp.zeros_like(r.grad_taps)
    strict = micro_order(lanes_of(MICRO)) < micro_order(rows_of(MICRO))
    blank = jnp.zeros((GROUP, WIDTH), F32)

    def summed(values, row):
        pick = (rows_of(8) == row).astype(BF16) + jnp.zeros((8, values.shape[1]), BF16)
        return dot(pick, values, (1, 1))

    def unit_back(head, group):
        columns, keeps = group_columns(r.table_t, group, heads)
        table = r.table[group]
        beta, growth, to_end = (columns[:, 4 * head + at : 4 * head + at + 1] for at in (0, 2, 3))
        decay = decay_of(columns, table, head, reach_of(columns, table))
        query, keys, values = r.query[head, group], r.key[head, group], r.value[head, group]
        keys_low, query_low = keys.astype(BF16), query.astype(BF16)
        solved, start = r.solved[head, group], r.starts[head, group]
        rows = pl.ds(pl.multiple_of(group * GROUP, GROUP), GROUP)
        grad_out = r.grad_mixed[rows, head * WIDTH : (head + 1) * WIDTH].astype(BF16)
        left = r.leaving[head, group]
        scores = r.scores[head, group]
        yield
        updates = solved[:, :WIDTH].astype(F32) - dot(solved[:, WIDTH:], start)
        carried = (to_end * keys).astype(BF16)
        grad_reach = dot(grad_out, start, (1, 1))
        grad_updates = dot(scores.astype(BF16), grad_out, (0, 0)) + dot(carried, left)
        yield
        updates = updates.astype(BF16)
        grad_scores = dot(grad_out, updates, (1, 1))
        grad_carried = dot(updates, left, (1, 1))
        grad_updates = grad_updates.astype(BF16)
        grad_pull = -dot(grad_updates, start, (1, 1))
        grad_total = jnp.sum(row_sum(start.astype(F32) * left.astype(F32)), axis=0, keepdims=True)
        yield
        both = jnp.concatenate([grad_updates, grad_pull.astype(BF16)], axis=1)
        right = dot(r.inverse[head, group], both, (0, 0))
        yield
        grad_lower = jnp.where(strict, -dot(right.astype(BF16), solved, (1, 1)), 0.0)
        right_value, right_key = right[:, :WIDTH], right[:, WIDTH:]
        grad_values = beta * right_value
        by_value = summed((right_value * values).astype(BF16), 0)
        by_key = summed((right_key * keys).astype(BF16), 1)
        by_end = summed((grad_carried * keys).astype(BF16), 3)
        yield
        pairs = (grad_scores * decay[GROUP:]).astype(BF16)
        grad_query = growth[GROUP:] * grad_reach + dot(pairs, keys_low)
        ratio = grad_lower * r.ratio[head, group]
        spread = ratio * beta
        grad_inner = (grad_lower * decay * beta).astype(BF16)
        yield
        grad_keys = (
            (beta * growth) * right_key
            + to_end * grad_carried
            + dot(pairs, query_low, (0, 0))
            + dot(grad_inner, keys_low)
            + dot(grad_inner, keys_low, (0, 0))
        )
        by_reach = summed(jnp.concatenate([blank, grad_reach * query], axis=0).astype(BF16), 4)
        spread = spread + jnp.concatenate([blank, grad_scores * scores], axis=0)
        spread = spread.astype(BF16)
        by_ratio = summed(ratio.astype(BF16), 2)
        by_row = summed(spread, 5)
        by_lane = dot(jnp.ones((8, MICRO), BF16), spread)
        yield
        lanes = by_value + by_key + by_ratio + by_end + by_reach + by_row
        at = 4 * head
        beta_lane, growth_lane, end_lane = (table[at + to : at + to + 1] for to in (0, 2, 3))
        is_last = lanes_of(MICRO) == MICRO - 1
        grad_beta = lanes[0:1] + lanes[1:2] * growth_lane + lanes[2:3]
        grad_growth = lanes[1:2] * beta_lane + lanes[4:5] + jnp.where(is_last, grad_total, 0.0)
        ended = lanes[3:4] * end_lane
        decayed = lanes[5:6] - by_lane[0:1] - ended + grad_growth * growth_lane
        decayed = decayed + jnp.where(is_last, row_sum(ended), 0.0)
        r.gate_rows[group, 2 * head : 2 * head + 2, :] = jnp.concatenate(
            [grad_beta, decayed], axis=0
        )
        yield
        grads = [
            grad_query,
            grad_keys[:GROUP],
            grad_keys[GROUP:],
            grad_values[:GROUP],
            grad_values[GROUP:],
        ]
        unit_rows = [query, keys[:GROUP], keys[GROUP:]]
        for part, grad in enumerate(grads):
            taps_at = head * channels + part * WIDTH
            taps_span = slice(taps_at, taps_at + WIDTH)
            taps = r.taps[:, taps_span]
            window = conv_window(r.proj, group, head * head_block + part * WIDTH)
            total = conv_total(window, keeps, taps)
            sigma = jax.nn.sigmoid(total)
            if part < 1 + HOUSE:
                mixed = total * sigma
                scale = lax.rsqrt(row_sum(mixed * mixed) + EPSILON)
                unit = unit_rows[part]
                grad = scale * (grad - unit * row_sum(grad * unit))
            grad = grad * sigma * (1.0 + total * (1.0 - sigma))
            moved_all = None
            taps_grads = []
            for step in range(4):
                kept = grad if step == 0 else grad * keeps[step]
                taps_grads.append(jnp.sum(kept * window[step], axis=0, keepdims=True))
                moved = kept * taps[step : step + 1]
                pieces = [jnp.zeros((8 - step, WIDTH), F32), moved]
                if step:
                    pieces.append(jnp.zeros((step, WIDTH), F32))
                moved = jnp.concatenate(pieces, axis=0)
                moved_all = moved if moved_all is None else moved_all + moved
            r.grad_taps[0:4, taps_span] += jnp.concatenate(taps_grads, axis=0)
            at = pl.ds(pl.multiple_of(group * GROUP + RIM - 8, 8), GROUP + 8)
            r.grad_conv[at, taps_span] += moved_all
            yield

    together = 2

    def run_units(head, turn):
        running = [unit_back(head, turn * together + extra) for extra in range(together)]
        while running:
            alive = []
            for unit in running:
                try:
                    next(unit)
                    alive.append(unit)
                except StopIteration:
                    pass
            running = alive

    def rim_back(head):
        lanes = pl.ds(head * channels, channels)
        return remote(
            r.grad_conv.at[pl.ds(RIM - 8, 8), lanes],
            r.rim_back.at[:, lanes],
            r.rim_sends.at[head],
            r.rim_receives.at[head],
            before,
        )

    for head in range(heads):
        name = "in%d" % head
        part_of[name] = SeqSum(
            getattr(r, "sum_" + name),
            getattr(r, "sides_" + name),
            getattr(r, "ups_" + name),
            getattr(r, "downs_" + name),
            r.sum_sends.at[4 + head],
            r.sum_receives.at[4 + head],
        )

    def finish_head(head):
        @pl.when(me_seq < n_seq - 1)
        def _():
            rim_back(head).wait_recv()

        lanes = slice(head * channels, (head + 1) * channels)
        came = jnp.where(me_seq < n_seq - 1, r.rim_back[:, lanes], 0.0)
        r.grad_conv[rows_here + RIM - 8 : rows_here + RIM, lanes] += came
        at = head * head_block
        r.grad_proj[:, at : at + channels] = r.grad_conv[RIM:, lanes].astype(BF16)
        part = slice(head * WIDTH, (head + 1) * WIDTH)
        r.grad_proj[:, at + channels : at + head_block] = r.grad_gate_part[:, part]
        name = "in%d" % head
        pair = 2 * depth
        for far in far_order(outer):
            features = slice(far * pair, (far + 1) * pair)
            found = dot(
                r.normed[RIM:, features], r.grad_proj[:, at : at + head_block], (0, 0)
            )
            getattr(r, "sum_" + name)[features, :] = found.astype(BF16)
            part_of[name].to_side(far).start()

    for head in range(heads):

        @pl.loop(0, groups // together)
        def _(turn):
            run_units(head, turn)

        @pl.when(me_seq > 0)
        def _():
            rim_back(head).start()

        if head == 0:
            part_of["down"].add_sides()
            for at in range(outer_head):
                out_sum.add_core(at)
            for step in range(1, outer_head):
                to_chip(0, r.out_cores, r.out_chips, step).start()
            need("grad_gate_part", "normed")
    for head in range(heads):
        finish_head(head)
        if head == 0:
            part_of["gate"].add_sides()
            part_of["down"].advance()

    need("logits", "w_small_all", "gain_one", "w_in_all", "rows", "grad_hidden", "grad_gain_two", "grad_gain_heads")
    logits = r.logits[...]
    sigma = jax.nn.sigmoid(logits)
    betas = 2.0 * sigma
    slopes = betas * (1.0 - 0.5 * betas)
    soft = soft_plus(logits)
    within = lanes_of(rows_here) & (GROUP - 1)
    pieces = []
    rate_grads = []
    for head in range(heads):
        line = lambda at: [r.gate_rows[group, 2 * head + at : 2 * head + at + 1, :] for group in range(groups)]
        beta_rows, decay_rows = line(0), line(1)
        at = head * (HOUSE + 1)
        for house in range(HOUSE):
            grad = jnp.concatenate(
                [row[:, house * GROUP : (house + 1) * GROUP] for row in beta_rows], axis=1
            )
            pieces.append(grad * slopes[at + house : at + house + 1])
        grad = jnp.concatenate([row[:, :GROUP] + row[:, GROUP:] for row in decay_rows], axis=1)
        step = 1
        while step < GROUP:
            moved = pltpu.roll(grad, rows_here - step, 1)
            grad = grad + jnp.where(within < GROUP - step, moved, 0.0)
            step *= 2
        at += HOUSE
        rate_grads.append(-jnp.sum(grad * soft[at : at + 1], axis=1, keepdims=True))
        pieces.append(-r.rate[head] * grad * sigma[at : at + 1])
    pieces.append(jnp.zeros((8 - len(pieces), rows_here), F32))
    grad_small = jnp.concatenate(pieces, axis=0).astype(BF16)
    grad_w_small = dot(grad_small, r.normed[RIM:, :])

    size = min(256, rows_here)
    ones = jnp.ones((8, model), BF16)
    for chunk in range(rows_here // size):
        rows = chunk_rows(chunk, size)
        back = dot(r.grad_proj[rows, :], r.w_in_all[...], (1, 1))
        back = back + dot(grad_small[:, chunk * size : (chunk + 1) * size], r.w_small_all[...], (0, 0))
        r.back_one[rows, :] = back.astype(BF16)
        weighted = back * r.gain_one[...] * r.rows[rows, :].astype(F32)
        high, low = halves(weighted)
        r.pulls[:, rows] = dot(ones, high, (1, 1)) + dot(ones, low, (1, 1))
    back_sum.start()
    pull_core = remote(
        r.pulls, r.pull_core, r.pull_sends.at[0], r.pull_receives.at[0], (me_seq, other_of(me_head))
    )
    pull_core.start()
    part_of["gate"].advance()
    part_of["down"].advance()
    for at in range(outer_head):
        back_sum.add_core(at)
    pull_core.wait()
    r.pull_core[...] += r.pulls[...]

    def pull_chip(step):
        return remote(
            r.pull_core,
            r.pull_chips.at[step],
            r.pull_sends.at[step],
            r.pull_receives.at[step],
            (me_seq, lax.rem(me_head + 2 * step, n_head)),
        )

    for step in range(1, outer_head):
        pull_chip(step).start()
        to_chip(1, r.back_cores, r.back_chips, step).start()
    for step in range(1, outer_head):
        to_chip(0, r.out_cores, r.out_chips, step).wait()
    value = r.hidden_own[...] + r.out_cores[chip].astype(F32)
    for step in range(1, outer_head):
        value = value + r.out_chips[step].astype(F32)
    r.result[...] = value.astype(BF16)
    part_of["up"].add_sides()
    part_of["gate"].advance()
    for step in range(1, outer_head):
        pull_chip(step).wait()
        to_chip(1, r.back_cores, r.back_chips, step).wait()
    pulls = r.pull_core[...]
    for step in range(1, outer_head):
        pulls = pulls + r.pull_chips[step]
    own = pl.ds(pl.multiple_of(me_head * span, span), span)
    gain_grad = jnp.zeros((1, span), F32)
    for chunk in range(rows_here // size):
        rows = chunk_rows(chunk, size)
        values = r.rows[rows, :].astype(F32)
        scale = lax.rsqrt(row_sum(values * values) / model + EPSILON)
        pull = jnp.transpose(pulls[:, chunk * size : (chunk + 1) * size])[:, 0:1]
        total = r.back_cores[chip, rows, :].astype(F32)
        for step in range(1, outer_head):
            total = total + r.back_chips[step, rows, :].astype(F32)
        mine = r.rows[rows, own].astype(F32)
        grad = scale * total * r.gain_one[:, own] - mine * (scale * scale * scale * pull / model)
        r.grad_inputs[rows, :] = grad + r.grad_hidden[rows, :]
        gain_grad = gain_grad + jnp.sum(total * mine * scale, axis=0, keepdims=True)
    part_of["up"].advance()

    gain_span, conv_span = span // n_seq, heads * channels // n_seq
    r.sum_tile[...] = jnp.zeros_like(r.sum_tile)
    for dest in range(n_seq):
        cut = slice(dest * gain_span, (dest + 1) * gain_span)
        at = dest * 16
        r.sum_tile[at : at + 1, 0:gain_span] = gain_grad[:, cut]
        r.sum_tile[at + 1 : at + 2, 0:gain_span] = r.grad_gain_two[:, cut]
        r.sum_tile[at + 2 : at + 3, 0:gain_span] = r.grad_gain_heads[:, cut]
        for head in range(heads):
            r.sum_tile[at + 3 : at + 4, head : head + 1] = rate_grads[head]
        r.sum_tile[at + 4 : at + 8, 0:conv_span] = r.grad_taps[
            0:4, dest * conv_span : (dest + 1) * conv_span
        ]
        r.sum_tile[at + 8 : at + 16, 0:depth] = grad_w_small[:, dest * depth : (dest + 1) * depth]
    tile_sum = SeqSum(
        r.sum_tile, r.sides_tile, r.ups_tile, r.downs_tile, r.sum_sends.at[4 + heads],
        r.sum_receives.at[4 + heads],
    )
    tile_sum.send_sides()
    part_of["out"].add_sides()
    part_of["up"].advance()
    part_of["out"].advance()
    part_of["down"].result(r.whole_units)
    r.grad_w_down[...] = jnp.transpose(r.whole_units[...])
    part_of["in0"].add_sides()
    part_of["out"].advance()
    part_of["gate"].result(r.whole_units)
    r.grad_w_gate_t[...] = jnp.transpose(r.whole_units[...])
    part_of["in0"].advance()
    tile_sum.add_sides()
    part_of["up"].result(r.whole_units)
    r.grad_w_up_t[...] = jnp.transpose(r.whole_units[...])
    for head in range(1, heads):
        part_of["in%d" % head].add_sides()
    part_of["in0"].advance()
    tile_sum.advance()
    part_of["out"].result(r.whole_out)
    r.grad_w_out[...] = jnp.transpose(r.whole_out[...])
    for head in range(1, heads):
        part_of["in%d" % head].advance()
    tile_sum.advance()
    for head in range(heads):
        lanes = pl.ds(head * head_block, head_block)
        part_of["in%d" % head].result(r.grad_w_in.at[:, lanes])
    tile_sum.result(r.small_sums)
    for each in list(part_of.values()) + [tile_sum]:
        each.finish()
    for head in range(heads):

        @pl.when(me_seq > 0)
        def _():
            rim_back(head).wait_send()

    @pl.when(place > 0)
    def _():
        step_down.wait_send()


def back_call(rate, kept, sizes):
    rows_here, model, block, heads, units, n_seq, n_head = sizes
    groups = rows_here // GROUP
    depth, span = model // n_seq, model // n_head
    outer, outer_head = n_seq // 2, n_head // 2
    own = heads * WIDTH
    channels = heads * (1 + 2 * HOUSE) * WIDTH
    lanes = -(-max(channels // n_seq, depth, WIDTH) // WIDTH) * WIDTH
    head_block = block // heads
    vmem = lambda dims, kind=F32: pltpu.VMEM(dims, kind)
    shapes = forward_shapes(*sizes)
    scratch = {name: vmem(*shapes[name]) for name in BACK_IN}
    widths = dict(down=units, gate=units, up=units, out=own)
    for head in range(heads):
        widths["in%d" % head] = head_block
    for name, width in widths.items():
        scratch["sum_" + name] = vmem((model, width), BF16)
        for way in ("sides_", "ups_", "downs_"):
            scratch[way + name] = vmem((outer, depth, width), BF16)
    scratch["sum_tile"] = vmem((n_seq * 16, lanes))
    for way in ("sides_", "ups_", "downs_"):
        scratch[way + "tile"] = vmem((outer, 16, lanes))
    square = (heads, WIDTH, WIDTH)
    scratch.update(
        own=vmem(square, BF16),
        theirs=vmem(square, BF16),
        moving=vmem(square, BF16),
        arriving=vmem(square, BF16),
        running=vmem(square),
        leaving=vmem((heads, groups, WIDTH, WIDTH), BF16),
        grad_conv=vmem((rows_here + RIM, channels)),
        grad_taps=vmem((8, channels)),
        gate_rows=vmem((groups, 8, MICRO)),
        rim_back=vmem((8, channels)),
        grad_proj=vmem((rows_here, block), BF16),
        back_one=vmem((rows_here, model), BF16),
        out_cores=vmem((outer_head, rows_here, span), BF16),
        out_chips=vmem((outer_head, rows_here, span), BF16),
        back_cores=vmem((outer_head, rows_here, span), BF16),
        back_chips=vmem((outer_head, rows_here, span), BF16),
        pulls=vmem((8, rows_here)),
        pull_core=vmem((8, rows_here)),
        pull_chips=vmem((outer_head, 8, rows_here)),
        whole_units=vmem((depth, units)),
        whole_out=vmem((depth, own)),
        loaded=DMA((len(BACK_IN),)),
        swap=DMA((4,)),
        sum_sends=DMA((5 + heads, 3, outer)),
        sum_receives=DMA((5 + heads, 3, outer)),
        core_sends=DMA((2, outer_head)),
        core_receives=DMA((2, outer_head)),
        chip_sends=DMA((2, outer_head)),
        chip_receives=DMA((2, outer_head)),
        pull_sends=DMA((outer_head,)),
        pull_receives=DMA((outer_head,)),
        rim_sends=DMA((heads,)),
        rim_receives=DMA((heads,)),
    )
    names = ["rate"] + ["in_" + name for name in BACK_IN] + BACK_OUT + list(scratch)
    outs = pl.pallas_call(
        partial(back_kernel, names, sizes),
        out_shape=[
            shape((rows_here, span), BF16),
            shape((rows_here, span), F32),
            shape((depth, block), F32),
            shape((units, depth), F32),
            shape((units, depth), F32),
            shape((units, depth), F32),
            shape((own, depth), F32),
            shape((16, lanes), F32),
        ],
        in_specs=[SMEM] + [ANY] * len(BACK_IN),
        out_specs=[VMEM] * len(BACK_OUT),
        scratch_shapes=list(scratch.values()),
        compiler_params=pltpu.CompilerParams(
            collective_id=1, has_side_effects=True, vmem_limit_bytes=VMEM_BYTES
        ),
        name="backward",
    )(rate, *[getattr(kept, name) for name in BACK_IN])
    return SimpleNamespace(**dict(zip(BACK_OUT, outs)))


def finish_kernel(small, *refs):
    ins, outs = refs[:8], refs[8:]
    for source, target in zip(ins[:7], outs[:7]):
        target[...] = source[...]
    sums = ins[7]
    for row in range(3):
        outs[7 + row][...] = sums[row : row + 1, 0 : outs[7 + row].shape[1]]
    outs[10][...] = sums[3:4, 0 : outs[10].shape[1]]
    outs[11][...] = sums[4:8, 0 : outs[11].shape[1]]
    outs[12][...] = sums[8 : 8 + small, 0 : outs[12].shape[1]]


def finish_call(out, gain_span, conv_span, depth, small, heads):
    arrays = [getattr(out, name) for name in BACK_OUT]
    shapes = [shape(a.shape, a.dtype) for a in arrays[:7]]
    shapes += [shape((1, gain_span), F32)] * 3
    shapes += [shape((1, heads), F32), shape((4, conv_span), F32), shape((small, depth), F32)]
    return pl.pallas_call(
        partial(finish_kernel, small),
        out_shape=shapes,
        in_specs=[VMEM] * 8,
        out_specs=[VMEM] * 13,
        compiler_params=pltpu.CompilerParams(vmem_limit_bytes=VMEM_BYTES),
        name="finish",
    )(*arrays)


def on_device(
    n_seq,
    n_head,
    inputs,
    lengths,
    norm1_gain,
    w_in,
    w_small,
    conv_weight,
    decay_rate,
    out_gain,
    w_out,
    norm2_gain,
    w_gate,
    w_up,
    w_down,
    cotangent,
):
    rows_here, span = inputs.shape
    heads = decay_rate.shape[0]
    small = w_small.shape[1]
    sizes = (rows_here, span * n_head, w_in.shape[1], heads, w_gate.shape[1], n_seq, n_head)
    gains = jnp.stack([norm1_gain, norm2_gain, out_gain]).astype(F32)
    kept = forward_call(
        (
            lengths,
            decay_rate,
            inputs,
            cotangent,
            gains,
            conv_weight,
            w_small.T,
            w_in,
            w_out,
            w_gate.T,
            w_up.T,
            w_down,
        ),
        sizes,
    )
    out = back_call(decay_rate, kept, sizes)
    gain_span, conv_span, depth = norm1_gain.shape[0], conv_weight.shape[1], w_in.shape[0]
    ends = finish_call(out, gain_span, conv_span, depth, small, heads)
    return (
        ends[0],
        ends[1],
        ends[7].reshape(-1),
        ends[2],
        ends[12].T,
        ends[11],
        ends[10].reshape(-1),
        ends[9].reshape(-1),
        ends[6],
        ends[8].reshape(-1),
        ends[3].T,
        ends[4].T,
        ends[5],
    )


def solution(mesh):
    return jax.shard_map(
        partial(on_device, mesh.shape["seq"], mesh.shape["head"]),
        mesh=mesh,
        in_specs=(
            P("seq", "head"),
            P(),
            P(("head", "seq")),
            P("seq", "head"),
            P("seq", "head"),
            P(None, ("head", "seq")),
            P("head"),
            P(("head", "seq")),
            P("head", "seq"),
            P(("head", "seq")),
            P("seq", "head"),
            P("seq", "head"),
            P("head", "seq"),
            P("seq", "head"),
        ),
        out_specs=(
            P("seq", "head"),
            P("seq", "head"),
            P(("head", "seq")),
            P("seq", "head"),
            P("seq", "head"),
            P(None, ("head", "seq")),
            P("head"),
            P(("head", "seq")),
            P("head", "seq"),
            P(("head", "seq")),
            P("seq", "head"),
            P("seq", "head"),
            P("head", "seq"),
        ),
        check_vma=False,
    )
```
